512 devices in a mesh: user: 128 (over z, y, core), ad: 4 (over x).
Axes of the slice: x: 4, y: 4, z: 16, core: 2. Of those that a mesh axis runs over, the one named last changes fastest.
Arguments:
- user_embedding: bfloat16 [32768, 128], P('user'), may hold values from -6 to 6
- user_scale: float32 [32768], P('user'), may hold values from 0.5 to 2
- user_mass: float32 [32768], P('user'), may hold values from 0.2 to 5
- ad_embedding: bfloat16 [16384, 128], P('ad'), may hold values from -6 to 6
- ad_scale: float32 [16384], P('ad'), may hold values from 0.5 to 2
- listing_view_demand: float32 [16384], P('ad'), may hold values from 0.2 to 5
- listing_unplaced_penalty: float32 [16384], P('ad'), may hold values from -2 to 2
- campaign_dual_vector_initial: float32 [16384], P(('ad', 'user')), may hold values from -6 to 6
- eligible: int32 [128, 4, 4], P('user', 'ad'), may hold values from 0 to 3, as said below
- counts: int32 [128, 4], P('user', 'ad'), may hold values from 1 to 4, as said below
Outputs:
- closing_viewer_scaling: float32 [32768], P('user')
- campaign_dual_vector_after: float32 [16384], P(('ad', 'user'))
The draws below stay inside these ranges and needn't reach their ends.
Inputs may be any that keep to these rules, and one draw needn't show every extreme that they name: The used entries of one list eligible[b, j, :] are distinct, and so are all 4 entries. `counts`: some pair (b, j) uses all 4 slots.
All inputs are finite; a program needn't handle non-finite values.
Results may differ from the reference program's by a relative error of at most 0.0003.
Values sent between devices are 32-bit elements; how exact they have to be, the bound alone decides.
No kernel may reach another device: no remote copies, remote signals or barrier semaphores. Data moves between devices by JAX's collectives and lax.ppermute only.
A program may use at most 64 MiB of HBM per device.

```python
import math
import jax
import jax.numpy as jnp
from jax import lax

E = 128
UBS = 256
ADS_IN_PART = 1024
AB_J = 4
KMAX = 4
ITERS = 2
UBLOCKS = 128
ADSHARDS = 4
USERS = 32768
ADS_J = 4096
ADS = 16384


def shared_lists(key):
    first_key, second_key = jax.random.split(jax.random.fold_in(key, 11))
    raw = jax.random.randint(first_key, (UBLOCKS, ADSHARDS, AB_J), 0, 1 << 20) * AB_J + jnp.arange(AB_J, dtype=jnp.int32)
    order = jnp.argsort(raw, axis=-1)[..., :KMAX].astype(jnp.int32)
    draws = jax.random.randint(second_key, (UBLOCKS, ADSHARDS), 0, 8)
    used = 1 + (draws >= 4).astype(jnp.int32) + (draws >= 6).astype(jnp.int32) + (draws >= 7).astype(jnp.int32)
    used = jnp.clip(used, 1, KMAX).astype(jnp.int32)
    used = used.at[0, 0].set(KMAX)
    return (order, used)


def shared_ads(key):
    values = jax.random.normal(jax.random.fold_in(key, 99), (ADS, E), jnp.float32)
    return jnp.clip(values, -6.0, 6.0)


def draw_eligible(key, part):
    order, used = shared_lists(key)
    return order


def draw_counts(key, part):
    order, used = shared_lists(key)
    return used


def draw_ad_embedding(key, part):
    values = shared_ads(key)
    return values.astype(jnp.bfloat16)


def draw_user_embedding(key, part):
    key = jax.random.fold_in(key, 7)
    values = jnp.clip(jax.random.normal(key, (USERS, E), jnp.float32), -6.0, 6.0)
    return values.astype(jnp.bfloat16)


def level_of(key, shape, pieces, least, largest):
    loudness, own = 1.0, jax.random.fold_in(key, 6)
    for position, shards_of in pieces:
        heights = jnp.exp(jax.random.uniform(jax.random.fold_in(own, position), (shards_of,), jnp.float32, least / len(pieces), largest / len(pieces)))
        loudness = loudness * jnp.repeat(heights, shape[position] // shards_of).reshape([-1 if axis == position else 1 for axis in range(len(shape))])
    return loudness


def bell_draw(rng, dims, spread, bound, cuts=(), kind=jnp.bfloat16):
    values = spread * jax.random.normal(rng, dims, jnp.float32)
    if cuts:
        values = values * level_of(rng, dims, cuts, -0.22, 0.18)
    return jnp.clip(values, -bound, bound).astype(kind)


def setup_inputs(seed: int = 0) -> dict:
    streams_of = jax.random.split(jax.random.key(seed), 11)
    user_embedding = draw_user_embedding(jax.random.fold_in(streams_of[10], 71), 0)
    user_scale = jnp.clip(jnp.exp(math.log(2.0) - 1.3862944 * jax.random.uniform(streams_of[1], (USERS,), jnp.float32) ** level_of(streams_of[1], (USERS,), ((0, 128),), -0.2, 0.2)), 0.5, 2.0)
    user_mass = jnp.clip(jnp.exp(math.log(5.0) - 3.218876 * jax.random.uniform(streams_of[2], (USERS,), jnp.float32) ** level_of(streams_of[2], (USERS,), ((0, 128),), -0.2, 0.2)), 0.2, 5.0)
    ad_embedding = draw_ad_embedding(jax.random.fold_in(streams_of[10], 71), 0)
    ad_scale = jnp.clip(jnp.exp(math.log(2.0) - 1.3862944 * jax.random.uniform(streams_of[4], (ADS,), jnp.float32) ** level_of(streams_of[4], (ADS,), ((0, 4),), -0.2, 0.2)), 0.5, 2.0)
    listing_view_demand = jnp.clip(jnp.exp(math.log(5.0) - 3.218876 * jax.random.uniform(streams_of[5], (ADS,), jnp.float32) ** level_of(streams_of[5], (ADS,), ((0, 4),), -0.2, 0.2)), 0.2, 5.0)
    listing_unplaced_penalty = jnp.clip(jax.random.uniform(streams_of[6], (ADS,), jnp.float32, -2.0, 2.0) * level_of(streams_of[6], (ADS,), ((0, 4),), -0.4, 0.0), -2.0, 2.0)
    campaign_dual_vector_initial = bell_draw(streams_of[7], (ADS,), 1.0, 6.0, ((0, 512),), jnp.float32)
    eligible = draw_eligible(jax.random.fold_in(streams_of[10], 71), 0)
    counts = draw_counts(jax.random.fold_in(streams_of[10], 71), 0)
    return dict(user_embedding=user_embedding, user_scale=user_scale, user_mass=user_mass, ad_embedding=ad_embedding, ad_scale=ad_scale, listing_view_demand=listing_view_demand, listing_unplaced_penalty=listing_unplaced_penalty, campaign_dual_vector_initial=campaign_dual_vector_initial, eligible=eligible, counts=counts)


regularizer_epsilon = 0.1
very_low = -1e+30

def pair_combine(first, second):
    ongoing_largest = jnp.maximum(first[0], second[0])
    return (ongoing_largest, first[1] * jnp.exp(first[0] - ongoing_largest) + second[1] * jnp.exp(second[0] - ongoing_largest))

def tile_cost(embed_rows, row_scale, ad_rows, ad_rowscale):
    product = jnp.dot(embed_rows.astype(jnp.float32), ad_rows.astype(jnp.float32).T, precision=lax.Precision.HIGHEST)
    return -(row_scale[:, None] * ad_rowscale[None, :]) * (product * (1.0 / math.sqrt(E)))

def reference(user_embedding, user_scale, user_mass, ad_embedding, ad_scale, listing_view_demand, listing_unplaced_penalty, campaign_dual_vector_initial, eligible, counts):
    user_blocks = user_embedding.reshape(UBLOCKS, UBS, E)
    scale_blocks = user_scale.reshape(UBLOCKS, UBS)
    mass_blocks = jnp.log(user_mass).reshape(UBLOCKS, UBS)
    ad_groups = ad_embedding.reshape(ADSHARDS, ADS_J, E)
    adscale_groups = ad_scale.reshape(ADSHARDS, ADS_J)
    lagrange_multiplier = campaign_dual_vector_initial
    closing_viewer_scaling = jnp.zeros((USERS,), jnp.float32)
    for sweep in range(ITERS):
        pot_groups = lagrange_multiplier.reshape(ADSHARDS, ADS_J)

        def one_block(carry, inputs):
            col_peak, col_total = carry
            embed_rows, row_scale, log_weight_share, partition_sequence, used = inputs
            tile_blocks = []
            source_largest_entry = jnp.full((UBS,), very_low, jnp.float32)
            source_exponent_accum = jnp.zeros((UBS,), jnp.float32)
            for group in range(ADSHARDS):
                for partition_index in range(KMAX):
                    offset = (partition_sequence[group, partition_index] * ADS_IN_PART).astype(jnp.int32)
                    ad_rows = lax.dynamic_slice_in_dim(ad_groups[group], offset, ADS_IN_PART, 0)
                    ad_rowscale = lax.dynamic_slice_in_dim(adscale_groups[group], offset, ADS_IN_PART, 0)
                    shipping_price = tile_cost(embed_rows, row_scale, ad_rows, ad_rowscale)
                    tile_blocks.append(shipping_price)
                    target_side_scaling = lax.dynamic_slice_in_dim(pot_groups[group], offset, ADS_IN_PART, 0)
                    affinity_table_entries = (target_side_scaling[None, :] - shipping_price) / regularizer_epsilon
                    tile_peak = lax.optimization_barrier(jnp.max(affinity_table_entries, axis=1))
                    tile_total = lax.optimization_barrier(jnp.sum(jnp.exp(affinity_table_entries - tile_peak[:, None]), axis=1))
                    new_peak, new_total = pair_combine((source_largest_entry, source_exponent_accum), (tile_peak, tile_total))
                    active = partition_index < used[group]
                    source_largest_entry = jnp.where(active, new_peak, source_largest_entry)
                    source_exponent_accum = jnp.where(active, new_total, source_exponent_accum)
            scaling_each_group = regularizer_epsilon * log_weight_share - regularizer_epsilon * (source_largest_entry + jnp.log(source_exponent_accum))
            for group in range(ADSHARDS):
                for partition_index in range(KMAX):
                    offset = (partition_sequence[group, partition_index] * ADS_IN_PART).astype(jnp.int32)
                    shipping_price = tile_blocks[group * KMAX + partition_index]
                    affinity_table_entries = (scaling_each_group[:, None] - shipping_price) / regularizer_epsilon
                    tile_peak = lax.optimization_barrier(jnp.max(affinity_table_entries, axis=0))
                    tile_total = lax.optimization_barrier(jnp.sum(jnp.exp(affinity_table_entries - tile_peak[None, :]), axis=0))
                    old_peak = lax.dynamic_slice_in_dim(col_peak[group], offset, ADS_IN_PART, 0)
                    old_total = lax.dynamic_slice_in_dim(col_total[group], offset, ADS_IN_PART, 0)
                    new_peak, new_total = pair_combine((old_peak, old_total), (tile_peak, tile_total))
                    active = partition_index < used[group]
                    new_peak = jnp.where(active, new_peak, old_peak)
                    new_total = jnp.where(active, new_total, old_total)
                    col_peak = col_peak.at[group].set(lax.dynamic_update_slice_in_dim(col_peak[group], new_peak, offset, 0))
                    col_total = col_total.at[group].set(lax.dynamic_update_slice_in_dim(col_total[group], new_total, offset, 0))
            return ((col_peak, col_total), scaling_each_group)
        start_carry = (jnp.full((ADSHARDS, ADS_J), very_low, jnp.float32), jnp.zeros((ADSHARDS, ADS_J), jnp.float32))
        (col_peak, col_total), block_pots = lax.scan(one_block, start_carry, (user_blocks, scale_blocks, mass_blocks, eligible, counts))
        closing_viewer_scaling = block_pots.reshape(USERS)
        fallback_affinity_level = -listing_unplaced_penalty / regularizer_epsilon
        ongoing_largest, ongoing_accumulation = pair_combine((col_peak.reshape(ADS), col_total.reshape(ADS)), (fallback_affinity_level, jnp.ones_like(fallback_affinity_level)))
        lagrange_multiplier = regularizer_epsilon * jnp.log(listing_view_demand) - regularizer_epsilon * (ongoing_largest + jnp.log(ongoing_accumulation))
    return (closing_viewer_scaling, lagrange_multiplier)
```

```python
import functools
import math

import jax
import jax.numpy as jnp
from jax import lax
from jax.experimental import pallas as pl
from jax.experimental.pallas import tpu as pltpu
from jax.sharding import Mesh
from jax.sharding import PartitionSpec as P

ADS_IN_PART = 1024
AB_J = 4
KMAX = 4
UBS = 256
NZ, NY, NC, NX = 16, 4, 2, 4
NS = NY * NC
NROW = NS * NX
SHARD = 32
USERS_HERE = NS * UBS
ADS_HERE = NZ * SHARD
PART_HERE = ADS_HERE // AB_J
ROWS = UBS + 8

regularizer_epsilon = 0.1
very_low = -1e30
LOG2E = math.log2(math.e)
TO_BITS = LOG2E / regularizer_epsilon
FROM_BITS = regularizer_epsilon / LOG2E
COL_SHIFT = 64.0
ROW_SHIFT = 100.0

VMEM_LIMIT = 40 * 1024 * 1024


def as_columns(row):
    return jnp.broadcast_to(row, (128, row.shape[1])).T


def tile_kernel(msg, ads, ad_weight, pot, tile, row_lse):
    weight = as_columns(ad_weight[...])
    pots = as_columns(pot[...])

    def block(s, carry):
        users = msg[s, :UBS, :].astype(jnp.bfloat16)
        scale = jnp.concatenate([msg[s, UBS : UBS + 1, :], msg[s, UBS + 1 : UBS + 2, :]], axis=1)
        at = pl.ds(pl.multiple_of(s * UBS, UBS), UBS)
        peaks, totals = [], []
        for q in range(AB_J):
            rows = slice(q * PART_HERE, (q + 1) * PART_HERE)
            product = lax.dot_general(
                ads[rows, :], users, (((1,), (1,)), ((), ())), preferred_element_type=jnp.float32
            )
            bias = msg[s, UBS + 4 + q : UBS + 5 + q, :]
            bias = jnp.concatenate([bias, bias], axis=1)
            wide = jnp.concatenate([weight[rows], weight[rows]], axis=1)
            values = product * wide * scale + bias
            tile[rows, at] = values
            values = values + jnp.concatenate([pots[rows], pots[rows]], axis=1)
            peak = jnp.max(values, axis=0, keepdims=True)
            peaks.append(peak)
            totals.append(jnp.sum(jnp.exp2(values - peak), axis=0, keepdims=True))
        peak = functools.reduce(jnp.maximum, peaks)
        total = sum(t * jnp.exp2(p - peak) for p, t in zip(peaks, totals))
        lse = peak + jnp.log2(total)
        row_lse[:, :, at] = jnp.broadcast_to(lse[None], (NROW, 1, UBS))
        return carry

    lax.fori_loop(0, NS, block, 0)


def column_sums(tile, row_pot, pots):
    sums = []
    for q in range(AB_J):
        rows = slice(q * PART_HERE, (q + 1) * PART_HERE)
        total = jnp.zeros((PART_HERE, 128), jnp.float32)
        for t in range(USERS_HERE // 128):
            lanes = slice(t * 128, (t + 1) * 128)
            total = total + jnp.exp2(tile[rows, lanes] + row_pot[:, lanes] + pots[rows])
        sums.append(jnp.sum(total.T, axis=0, keepdims=True))
    return jnp.concatenate(sums, axis=1)


def log_mass_of(msg):
    return jnp.concatenate(
        [msg[s, UBS + 2 + h : UBS + 3 + h, :] for s in range(NS) for h in range(2)], axis=1
    )


def first_column_kernel(tile, parts, mass, pot, row_pot_out, col_out):
    peak = jnp.max(parts[...], axis=0)
    total = jnp.sum(jnp.exp2(parts[...] - peak[None]), axis=0)
    row_pot = mass[...] - (peak + jnp.log2(total))
    row_pot_out[...] = row_pot
    sums = column_sums(tile, row_pot + COL_SHIFT, as_columns(pot[...]))
    col_out[...] = jnp.broadcast_to(sums[None], (NZ, 1, ADS_HERE))


def column_update(log_sum, fallback, log_demand):
    peak = jnp.maximum(log_sum, fallback)
    return log_demand - (peak + jnp.log2(jnp.exp2(log_sum - peak) + jnp.exp2(fallback - peak)))


def second_row_kernel(tile, parts, row_pot, pot, fallback, log_demand, pot_out, row_out):
    sums = jnp.sum(parts[...], axis=0)
    new_pot = column_update(
        jnp.log2(sums) - COL_SHIFT - pot[...], fallback[...], log_demand[...]
    )
    pot_out[...] = new_pot
    pots = as_columns(new_pot)
    for t in range(USERS_HERE // 128):
        lanes = slice(t * 128, (t + 1) * 128)
        shift = row_pot[:, lanes] + ROW_SHIFT
        total = jnp.zeros((8, 128), jnp.float32)
        for q in range(AB_J):
            rows = slice(q * PART_HERE, (q + 1) * PART_HERE)
            terms = jnp.exp2(tile[rows, lanes] + shift + pots[rows])
            total = total + jnp.sum(terms.reshape(PART_HERE // 8, 8, 128), axis=0)
        total = jnp.sum(total, axis=0, keepdims=True)
        row_out[:, :, lanes] = jnp.broadcast_to(total[None], (NROW, 1, 128))


def second_column_kernel(own, tile, parts, row_pot, mass, pot, user_out, col_out):
    sums = jnp.sum(parts[...], axis=0)
    new = row_pot[...] + (mass[...] + ROW_SHIFT - jnp.log2(sums))
    col_out[...] = column_sums(tile, new, as_columns(pot[...]))
    picked = jnp.zeros((1, UBS), jnp.float32)
    for s in range(NS):
        picked = jnp.where(own[0] == s, new[:, s * UBS : (s + 1) * UBS], picked)
    user_out[...] = picked * FROM_BITS


def last_kernel(parts, pot, fallback, log_demand, out):
    sums = jnp.sum(parts[...], axis=0)
    out[...] = (
        column_update(jnp.log2(sums) - pot[...], fallback[...], log_demand[...]) * FROM_BITS
    )


def call(kernel, out_shape, *operands, scalars=0):
    vmem = pl.BlockSpec(memory_space=pltpu.VMEM)
    smem = pl.BlockSpec(memory_space=pltpu.SMEM)
    return pl.pallas_call(
        kernel,
        out_shape=[jax.ShapeDtypeStruct(s, jnp.float32) for s in out_shape],
        in_specs=[smem] * scalars + [vmem] * (len(operands) - scalars),
        out_specs=[vmem] * len(out_shape),
        compiler_params=pltpu.CompilerParams(vmem_limit_bytes=VMEM_LIMIT),
    )(*operands)


def to_all(value, axes, count):
    return lax.all_to_all(
        jnp.broadcast_to(value[None], (count,) + value.shape), axes, 0, 0, tiled=True
    )


def on_device(
    user_embedding,
    user_scale,
    user_mass,
    ad_embedding,
    ad_scale,
    listing_view_demand,
    listing_unplaced_penalty,
    campaign_dual_vector_initial,
    eligible,
    counts,
):
    inverse_root = 1.0 / math.sqrt(user_embedding.shape[1])
    mine = lax.axis_index("y") * NC + lax.axis_index("c")

    used = jnp.arange(KMAX) < counts[0, 0]
    active = jnp.any(
        (eligible[0, 0][None, :] == jnp.arange(AB_J)[:, None]) & used[None, :], axis=1
    )
    bias = jnp.where(active, 0.0, very_low).astype(jnp.float32)
    message = jnp.concatenate(
        [
            user_embedding.astype(jnp.float32),
            user_scale.reshape(2, 128),
            jnp.log2(user_mass).reshape(2, 128),
            jnp.broadcast_to(bias[:, None], (AB_J, 128)),
        ]
    )
    messages = to_all(message, ("y", "c"), NS)
    pot = to_all(campaign_dual_vector_initial * TO_BITS, "z", NZ).reshape(1, ADS_HERE)

    def of_here(array):
        shape = array.shape[1:]
        picked = lax.dynamic_index_in_dim(
            array.reshape((NZ, NS, SHARD) + shape), mine, 1, keepdims=False
        )
        return picked.reshape((ADS_HERE,) + shape)

    ads = of_here(ad_embedding)
    weight = (of_here(ad_scale) * (inverse_root * TO_BITS)).reshape(1, ADS_HERE)
    fallback = (of_here(listing_unplaced_penalty) * -TO_BITS).reshape(1, ADS_HERE)
    log_demand = jnp.log2(of_here(listing_view_demand)).reshape(1, ADS_HERE)
    mass = messages[:, UBS + 2 : UBS + 4, :].reshape(1, USERS_HERE)

    row_axes = ("y", "c", "x")
    tile, row_parts = call(
        tile_kernel,
        [(ADS_HERE, USERS_HERE), (NROW, 1, USERS_HERE)],
        messages, ads, weight, pot,
    )
    row_parts = lax.all_to_all(row_parts, row_axes, 0, 0, tiled=True)
    row_pot, col_parts = call(
        first_column_kernel,
        [(1, USERS_HERE), (NZ, 1, ADS_HERE)],
        tile, row_parts, mass, pot,
    )
    col_parts = lax.all_to_all(col_parts, "z", 0, 0, tiled=True)
    pot, row_parts = call(
        second_row_kernel,
        [(1, ADS_HERE), (NROW, 1, USERS_HERE)],
        tile, col_parts, row_pot, pot, fallback, log_demand,
    )
    row_parts = lax.all_to_all(row_parts, row_axes, 0, 0, tiled=True)
    users, col_parts = call(
        second_column_kernel,
        [(1, UBS), (1, ADS_HERE)],
        mine.reshape(1), tile, row_parts, row_pot, mass, pot,
        scalars=1,
    )
    col_parts = lax.all_to_all(col_parts.reshape(NZ, 1, SHARD), "z", 0, 0, tiled=True)

    def of_mine(row):
        return lax.dynamic_slice_in_dim(row, lax.axis_index("z") * SHARD, SHARD, 1)

    (last,) = call(
        last_kernel, [(1, SHARD)],
        col_parts, of_mine(pot), of_mine(fallback), of_mine(log_demand),
    )
    return users.reshape(UBS), last.reshape(SHARD)


def solution(mesh):
    fine = Mesh(mesh.devices.reshape(NZ, NY, NC, NX), ("z", "y", "c", "x"))
    user = ("z", "y", "c")
    in_specs = (
        P(user, None),
        P(user),
        P(user),
        P("x", None),
        P("x"),
        P("x"),
        P("x"),
        P(("x",) + user),
        P(user, "x", None),
        P(user, "x"),
    )
    out_specs = (P(user), P(("x",) + user))
    return jax.shard_map(
        on_device, mesh=fine, in_specs=in_specs, out_specs=out_specs, check_vma=False
    )
```

```python
import functools
import math

import jax
import jax.numpy as jnp
from jax import lax
from jax.experimental import pallas as pl
from jax.experimental.pallas import tpu as pltpu
from jax.sharding import Mesh
from jax.sharding import PartitionSpec as P

ADS_IN_PART = 1024
AB_J = 4
KMAX = 4
UBS = 256
NZ, NY, NC, NX = 16, 4, 2, 4
NS = NY * NC
NROW = NS * NX
SHARD = 32
USERS_HERE = NS * UBS
ADS_HERE = NZ * SHARD
PART_HERE = ADS_HERE // AB_J
ROWS = UBS + 8

regularizer_epsilon = 0.1
very_low = -1e30
LOG2E = math.log2(math.e)
TO_BITS = LOG2E / regularizer_epsilon
FROM_BITS = regularizer_epsilon / LOG2E
COL_SHIFT = 64.0
ROW_SHIFT = 100.0

VMEM_LIMIT = 40 * 1024 * 1024


def as_columns(row):
    return jnp.broadcast_to(row, (128, row.shape[1])).T


def message_kernel(eligible, counts, embedding, scale, mass, out):
    out[:UBS, :] = embedding[...].astype(jnp.float32)
    out[UBS : UBS + 2, :] = scale[...]
    out[UBS + 2 : UBS + 4, :] = jnp.log2(mass[...])
    for q in range(AB_J):
        bias = jnp.float32(very_low)
        for k in range(KMAX):
            hit = jnp.logical_and(k < counts[0, 0], eligible[0, 0, k] == q)
            bias = jnp.where(hit, jnp.float32(0.0), bias)
        out[UBS + 4 + q : UBS + 5 + q, :] = jnp.full((1, 128), bias, jnp.float32)


def tile_kernel(
    mine, msg0, msg1, msg2, msg3, ads, ad_weight, pot_parts, fallback, log_demand,
    tile, row_lse, log_mass, pot,
):
    del fallback, log_demand
    weight = as_columns(ad_weight[...])
    pots = jnp.concatenate(
        [jnp.sum(pot_parts[4 * q : 4 * q + 4], axis=0) for q in range(AB_J)], axis=1
    )
    pot[...] = pots
    pots = as_columns(pots)
    for back, msg in enumerate((msg0, msg1, msg2, msg3)):
        first = lax.rem(mine[0] + (NY - back), NY) * NC

        def block(c, carry, msg=msg, first=first):
            users = msg[c, :UBS, :].astype(jnp.bfloat16)
            scale = jnp.concatenate(
                [msg[c, UBS : UBS + 1, :], msg[c, UBS + 1 : UBS + 2, :]], axis=1
            )
            at = pl.ds(pl.multiple_of((first + c) * UBS, UBS), UBS)
            log_mass[:, at] = jnp.concatenate(
                [msg[c, UBS + 2 : UBS + 3, :], msg[c, UBS + 3 : UBS + 4, :]], axis=1
            )
            peaks, totals = [], []
            for q in range(AB_J):
                rows = slice(q * PART_HERE, (q + 1) * PART_HERE)
                product = lax.dot_general(
                    ads[rows, :], users, (((1,), (1,)), ((), ())),
                    preferred_element_type=jnp.float32,
                )
                bias = msg[c, UBS + 4 + q : UBS + 5 + q, :]
                bias = jnp.concatenate([bias, bias], axis=1)
                wide = jnp.concatenate([weight[rows], weight[rows]], axis=1)
                values = product * wide * scale + bias
                tile[rows, at] = values
                values = values + jnp.concatenate([pots[rows], pots[rows]], axis=1)
                peak = jnp.max(values, axis=0, keepdims=True)
                peaks.append(peak)
                totals.append(jnp.sum(jnp.exp2(values - peak), axis=0, keepdims=True))
            peak = functools.reduce(jnp.maximum, peaks)
            total = sum(t * jnp.exp2(p - peak) for p, t in zip(peaks, totals))
            lse = peak + jnp.log2(total)
            row_lse[:, :, at] = jnp.broadcast_to(lse[None], (NROW, 1, UBS))
            return carry

        lax.fori_loop(0, NC, block, 0)


def column_sums(tile, row_pot, pots):
    sums = []
    for q in range(AB_J):
        rows = slice(q * PART_HERE, (q + 1) * PART_HERE)
        total = jnp.zeros((PART_HERE, 128), jnp.float32)
        for t in range(USERS_HERE // 128):
            lanes = slice(t * 128, (t + 1) * 128)
            total = total + jnp.exp2(tile[rows, lanes] + row_pot[:, lanes] + pots[rows])
        sums.append(jnp.sum(total.T, axis=0, keepdims=True))
    return jnp.concatenate(sums, axis=1)


def first_column_kernel(tile, parts, mass, pot, row_pot_out, col_out):
    peak = jnp.max(parts[...], axis=0)
    total = jnp.sum(jnp.exp2(parts[...] - peak[None]), axis=0)
    row_pot = mass[...] - (peak + jnp.log2(total))
    row_pot_out[...] = row_pot
    sums = column_sums(tile, row_pot + COL_SHIFT, as_columns(pot[...]))
    col_out[...] = jnp.broadcast_to(sums[None], (NZ, 1, ADS_HERE))


def column_update(log_sum, fallback, log_demand):
    peak = jnp.maximum(log_sum, fallback)
    return log_demand - (peak + jnp.log2(jnp.exp2(log_sum - peak) + jnp.exp2(fallback - peak)))


def second_row_kernel(tile, parts, row_pot, pot, fallback, log_demand, pot_out, row_out):
    sums = jnp.sum(parts[...], axis=0)
    new_pot = column_update(
        jnp.log2(sums) - COL_SHIFT - pot[...], fallback[...], log_demand[...]
    )
    pot_out[...] = new_pot
    pots = as_columns(new_pot)
    for t in range(USERS_HERE // 128):
        lanes = slice(t * 128, (t + 1) * 128)
        shift = row_pot[:, lanes] + ROW_SHIFT
        total = jnp.zeros((8, 128), jnp.float32)
        for q in range(AB_J):
            rows = slice(q * PART_HERE, (q + 1) * PART_HERE)
            terms = jnp.exp2(tile[rows, lanes] + shift + pots[rows])
            total = total + jnp.sum(terms.reshape(PART_HERE // 8, 8, 128), axis=0)
        total = jnp.sum(total, axis=0, keepdims=True)
        row_out[:, :, lanes] = jnp.broadcast_to(total[None], (NROW, 1, 128))


def second_column_kernel(own, tile, parts, row_pot, mass, pot, user_out, col_out):
    sums = jnp.sum(parts[...], axis=0)
    new = row_pot[...] + (mass[...] + ROW_SHIFT - jnp.log2(sums))
    sums = column_sums(tile, new, as_columns(pot[...]))
    col_out[...] = jnp.broadcast_to(sums[None], (NZ, 1, ADS_HERE))
    picked = jnp.zeros((1, UBS), jnp.float32)
    for s in range(NS):
        picked = jnp.where(own[0] == s, new[:, s * UBS : (s + 1) * UBS], picked)
    user_out[...] = picked * FROM_BITS


def last_kernel(own, parts, pot, fallback, log_demand, out):
    sums = jnp.sum(parts[...], axis=0)
    new = column_update(jnp.log2(sums) - pot[...], fallback[...], log_demand[...]) * FROM_BITS
    new = jnp.broadcast_to(new, (8, ADS_HERE))
    turned = pltpu.roll(new, lax.rem(ADS_HERE - own[0] * SHARD, ADS_HERE), 1)
    out[...] = turned[:1, :SHARD]


def call(kernel, out_shape, *operands, scalars=0):
    vmem = pl.BlockSpec(memory_space=pltpu.VMEM)
    smem = pl.BlockSpec(memory_space=pltpu.SMEM)
    return pl.pallas_call(
        kernel,
        out_shape=[jax.ShapeDtypeStruct(s, jnp.float32) for s in out_shape],
        in_specs=[smem] * scalars + [vmem] * (len(operands) - scalars),
        out_specs=[vmem] * len(out_shape),
        compiler_params=pltpu.CompilerParams(vmem_limit_bytes=VMEM_LIMIT),
    )(*operands)


def on_device(
    user_embedding,
    user_scale,
    user_mass,
    ad_embedding,
    ad_scale,
    listing_view_demand,
    listing_unplaced_penalty,
    campaign_dual_vector_initial,
    eligible,
    counts,
):
    inverse_root = 1.0 / math.sqrt(user_embedding.shape[1])
    y, z = lax.axis_index("y"), lax.axis_index("z")
    mine = y * NC + lax.axis_index("c")

    pot_part = lax.dynamic_update_slice(
        jnp.zeros((128,), jnp.float32),
        campaign_dual_vector_initial * TO_BITS,
        (lax.rem(z, AB_J) * SHARD,),
    )
    pot_parts = lax.all_to_all(
        jnp.broadcast_to(pot_part, (NZ, 1, 128)), "z", 0, 0, tiled=True
    )

    (message,) = call(
        message_kernel,
        [(ROWS, 128)],
        eligible, counts, user_embedding, user_scale.reshape(2, 128), user_mass.reshape(2, 128),
        scalars=2,
    )
    pair = lax.all_gather(message, "c")
    messages = [pair] + [
        lax.ppermute(pair, "y", [(i, (i + d) % NY) for i in range(NY)]) for d in range(1, NY)
    ]

    def of_here(array):
        shape = array.shape[1:]
        picked = lax.dynamic_index_in_dim(
            array.reshape((NZ, NS, SHARD) + shape), mine, 1, keepdims=False
        )
        return picked.reshape((ADS_HERE,) + shape)

    ads = of_here(ad_embedding)
    weight = (of_here(ad_scale) * (inverse_root * TO_BITS)).reshape(1, ADS_HERE)
    fallback = (of_here(listing_unplaced_penalty) * -TO_BITS).reshape(1, ADS_HERE)
    log_demand = jnp.log2(of_here(listing_view_demand)).reshape(1, ADS_HERE)

    row_axes = ("y", "c", "x")
    tile, row_parts, mass, pot = call(
        tile_kernel,
        [(ADS_HERE, USERS_HERE), (NROW, 1, USERS_HERE), (1, USERS_HERE), (1, ADS_HERE)],
        y.reshape(1), *messages, ads, weight, pot_parts, fallback, log_demand,
        scalars=1,
    )
    row_parts = lax.all_to_all(row_parts, row_axes, 0, 0, tiled=True)
    row_pot, col_parts = call(
        first_column_kernel,
        [(1, USERS_HERE), (NZ, 1, ADS_HERE)],
        tile, row_parts, mass, pot,
    )
    col_parts = lax.all_to_all(col_parts, "z", 0, 0, tiled=True)
    pot, row_parts = call(
        second_row_kernel,
        [(1, ADS_HERE), (NROW, 1, USERS_HERE)],
        tile, col_parts, row_pot, pot, fallback, log_demand,
    )
    row_parts = lax.all_to_all(row_parts, row_axes, 0, 0, tiled=True)
    users, col_parts = call(
        second_column_kernel,
        [(1, UBS), (NZ, 1, ADS_HERE)],
        mine.reshape(1), tile, row_parts, row_pot, mass, pot,
        scalars=1,
    )
    col_parts = lax.all_to_all(col_parts, "z", 0, 0, tiled=True)
    (last,) = call(
        last_kernel, [(1, SHARD)],
        z.reshape(1), col_parts, pot, fallback, log_demand,
        scalars=1,
    )
    return users.reshape(UBS), last.reshape(SHARD)


def solution(mesh):
    fine = Mesh(mesh.devices.reshape(NZ, NY, NC, NX), ("z", "y", "c", "x"))
    user = ("z", "y", "c")
    in_specs = (
        P(user, None),
        P(user),
        P(user),
        P("x", None),
        P("x"),
        P("x"),
        P("x"),
        P(("x",) + user),
        P(user, "x", None),
        P(user, "x"),
    )
    out_specs = (P(user), P(("x",) + user))
    return jax.shard_map(
        on_device, mesh=fine, in_specs=in_specs, out_specs=out_specs, check_vma=False
    )
```

```python
import functools
import math

import jax
import jax.numpy as jnp
from jax import lax
from jax.experimental import pallas as pl
from jax.experimental.pallas import tpu as pltpu
from jax.sharding import Mesh
from jax.sharding import PartitionSpec as P

ADS_IN_PART = 1024
AB_J = 4
KMAX = 4
UBS = 256
NZ, NY, NC, NX = 16, 4, 2, 4
NS = NY * NC
NROW = NS * NX
SHARD = 32
USERS_HERE = NS * UBS
ADS_HERE = NZ * SHARD
PART_HERE = ADS_HERE // AB_J
ROWS = UBS + 8

regularizer_epsilon = 0.1
very_low = -1e30
LOG2E = math.log2(math.e)
TO_BITS = LOG2E / regularizer_epsilon
FROM_BITS = regularizer_epsilon / LOG2E
COL_SHIFT = 64.0
ROW_SHIFT = 100.0

VMEM_LIMIT = 40 * 1024 * 1024


def as_columns(row):
    return jnp.broadcast_to(row, (128, row.shape[1])).T


def message_kernel(
    eligible, counts, embedding, scale, mass, out, embedding_here, mass_here, sems
):
    copies = [
        pltpu.make_async_copy(embedding, embedding_here, sems.at[0]),
        pltpu.make_async_copy(scale, out.at[pl.ds(UBS, 2), :], sems.at[1]),
        pltpu.make_async_copy(mass, mass_here, sems.at[2]),
    ]
    for copy in copies:
        copy.start()
    for q in range(AB_J):
        bias = jnp.float32(very_low)
        for k in range(KMAX):
            hit = jnp.logical_and(k < counts[0, 0], eligible[0, 0, k] == q)
            bias = jnp.where(hit, jnp.float32(0.0), bias)
        out[UBS + 4 + q : UBS + 5 + q, :] = jnp.full((1, 128), bias, jnp.float32)
    for copy in copies:
        copy.wait()
    out[:UBS, :] = embedding_here[...].astype(jnp.float32)
    out[UBS + 2 : UBS + 4, :] = jnp.log2(mass_here[...])


def tile_kernel(
    mine, place, msg0, msg1, msg2, msg3, ads, ad_weight, pot_parts, fallback, log_demand,
    tile, row_lse, log_mass, pot,
):
    del place, fallback, log_demand
    weight = as_columns(ad_weight[...])
    pots = jnp.concatenate([pot_parts[z] for z in range(NZ)], axis=1) * TO_BITS
    pot[...] = pots
    pots = as_columns(pots)
    for back, msg in enumerate((msg0, msg1, msg2, msg3)):
        first = lax.rem(mine[0] + (NY - back), NY) * NC

        def block(c, carry, msg=msg, first=first):
            users = msg[c, :UBS, :].astype(jnp.bfloat16)
            scale = jnp.concatenate(
                [msg[c, UBS : UBS + 1, :], msg[c, UBS + 1 : UBS + 2, :]], axis=1
            )
            at = pl.ds(pl.multiple_of((first + c) * UBS, UBS), UBS)
            log_mass[:, at] = jnp.concatenate(
                [msg[c, UBS + 2 : UBS + 3, :], msg[c, UBS + 3 : UBS + 4, :]], axis=1
            )
            peaks, totals = [], []
            for q in range(AB_J):
                rows = slice(q * PART_HERE, (q + 1) * PART_HERE)
                product = lax.dot_general(
                    ads[rows, :], users, (((1,), (1,)), ((), ())),
                    preferred_element_type=jnp.float32,
                )
                bias = msg[c, UBS + 4 + q : UBS + 5 + q, :]
                bias = jnp.concatenate([bias, bias], axis=1)
                wide = jnp.concatenate([weight[rows], weight[rows]], axis=1)
                values = product * wide * scale + bias
                tile[rows, at] = values
                values = values + jnp.concatenate([pots[rows], pots[rows]], axis=1)
                peak = jnp.max(values, axis=0, keepdims=True)
                peaks.append(peak)
                totals.append(jnp.sum(jnp.exp2(values - peak), axis=0, keepdims=True))
            peak = functools.reduce(jnp.maximum, peaks)
            total = sum(t * jnp.exp2(p - peak) for p, t in zip(peaks, totals))
            lse = peak + jnp.log2(total)
            row_lse[:, :, at] = jnp.broadcast_to(lse[None], (NROW, 1, UBS))
            return carry

        lax.fori_loop(0, NC, block, 0)


def column_sums(tile, row_pot, pots):
    sums = []
    for q in range(AB_J):
        rows = slice(q * PART_HERE, (q + 1) * PART_HERE)
        total = jnp.zeros((PART_HERE, 128), jnp.float32)
        for t in range(USERS_HERE // 128):
            lanes = slice(t * 128, (t + 1) * 128)
            total = total + jnp.exp2(tile[rows, lanes] + row_pot[:, lanes] + pots[rows])
        sums.append(jnp.sum(total.T, axis=0, keepdims=True))
    return jnp.concatenate(sums, axis=1)


def first_column_kernel(tile, parts, mass, pot, row_pot_out, col_out):
    peak = jnp.max(parts[...], axis=0)
    total = jnp.sum(jnp.exp2(parts[...] - peak[None]), axis=0)
    row_pot = mass[...] - (peak + jnp.log2(total))
    row_pot_out[...] = row_pot
    sums = column_sums(tile, row_pot + COL_SHIFT, as_columns(pot[...]))
    col_out[...] = jnp.broadcast_to(sums[None], (NZ, 1, ADS_HERE))


def column_update(log_sum, fallback, log_demand):
    peak = jnp.maximum(log_sum, fallback)
    return log_demand - (peak + jnp.log2(jnp.exp2(log_sum - peak) + jnp.exp2(fallback - peak)))


def second_row_kernel(tile, parts, row_pot, pot, fallback, log_demand, pot_out, row_out):
    sums = jnp.sum(parts[...], axis=0)
    new_pot = column_update(
        jnp.log2(sums) - COL_SHIFT - pot[...], fallback[...], log_demand[...]
    )
    pot_out[...] = new_pot
    pots = as_columns(new_pot)
    for t in range(USERS_HERE // 128):
        lanes = slice(t * 128, (t + 1) * 128)
        shift = row_pot[:, lanes] + ROW_SHIFT
        total = jnp.zeros((8, 128), jnp.float32)
        for q in range(AB_J):
            rows = slice(q * PART_HERE, (q + 1) * PART_HERE)
            terms = jnp.exp2(tile[rows, lanes] + shift + pots[rows])
            total = total + jnp.sum(terms.reshape(PART_HERE // 8, 8, 128), axis=0)
        total = jnp.sum(total, axis=0, keepdims=True)
        row_out[:, :, lanes] = jnp.broadcast_to(total[None], (NROW, 1, 128))


def second_column_kernel(own, tile, parts, row_pot, mass, pot, user_out, col_out):
    sums = jnp.sum(parts[...], axis=0)
    new = row_pot[...] + (mass[...] + ROW_SHIFT - jnp.log2(sums))
    sums = column_sums(tile, new, as_columns(pot[...]))
    col_out[...] = jnp.broadcast_to(sums[None], (NZ, 1, ADS_HERE))
    picked = jnp.zeros((1, UBS), jnp.float32)
    for s in range(NS):
        picked = jnp.where(own[0] == s, new[:, s * UBS : (s + 1) * UBS], picked)
    user_out[...] = picked * FROM_BITS


def last_kernel(own, parts, pot, fallback, log_demand, out):
    sums = jnp.sum(parts[...], axis=0)
    new = column_update(jnp.log2(sums) - pot[...], fallback[...], log_demand[...]) * FROM_BITS
    new = jnp.broadcast_to(new, (8, ADS_HERE))
    turned = pltpu.roll(new, lax.rem(ADS_HERE - own[0] * SHARD, ADS_HERE), 1)
    out[...] = turned[:1, :SHARD]


def call(kernel, out_shape, *operands, scalars=0):
    vmem = pl.BlockSpec(memory_space=pltpu.VMEM)
    smem = pl.BlockSpec(memory_space=pltpu.SMEM)
    return pl.pallas_call(
        kernel,
        out_shape=[jax.ShapeDtypeStruct(s, jnp.float32) for s in out_shape],
        in_specs=[smem] * scalars + [vmem] * (len(operands) - scalars),
        out_specs=[vmem] * len(out_shape),
        compiler_params=pltpu.CompilerParams(vmem_limit_bytes=VMEM_LIMIT),
    )(*operands)


def on_device(
    user_embedding,
    user_scale,
    user_mass,
    ad_embedding,
    ad_scale,
    listing_view_demand,
    listing_unplaced_penalty,
    campaign_dual_vector_initial,
    eligible,
    counts,
):
    inverse_root = 1.0 / math.sqrt(user_embedding.shape[1])
    y, z = lax.axis_index("y"), lax.axis_index("z")
    mine = y * NC + lax.axis_index("c")

    pot_parts = lax.all_to_all(
        jnp.broadcast_to(campaign_dual_vector_initial, (NZ, 1, SHARD)), "z", 0, 0, tiled=True
    )

    message = pl.pallas_call(
        message_kernel,
        out_shape=jax.ShapeDtypeStruct((ROWS, 128), jnp.float32),
        in_specs=[pl.BlockSpec(memory_space=pltpu.SMEM)] * 2
        + [pl.BlockSpec(memory_space=pl.ANY)] * 3,
        out_specs=pl.BlockSpec(memory_space=pltpu.VMEM),
        scratch_shapes=[
            pltpu.VMEM((UBS, 128), jnp.bfloat16),
            pltpu.VMEM((2, 128), jnp.float32),
            pltpu.SemaphoreType.DMA((3,)),
        ],
    )(eligible, counts, user_embedding, user_scale.reshape(2, 128), user_mass.reshape(2, 128))
    messages = [
        lax.ppermute(message, "y", [(i, (i + d) % NY) for i in range(NY)]) for d in range(1, NY)
    ]
    messages = [lax.all_gather(m, "c") for m in [message] + messages]

    def of_here(array):
        shape = array.shape[1:]
        picked = lax.dynamic_index_in_dim(
            array.reshape((NZ, NS, SHARD) + shape), mine, 1, keepdims=False
        )
        return picked.reshape((ADS_HERE,) + shape)

    ads = of_here(ad_embedding)
    weight = (of_here(ad_scale) * (inverse_root * TO_BITS)).reshape(1, ADS_HERE)
    fallback = (of_here(listing_unplaced_penalty) * -TO_BITS).reshape(1, ADS_HERE)
    log_demand = jnp.log2(of_here(listing_view_demand)).reshape(1, ADS_HERE)

    row_axes = ("y", "c", "x")
    tile, row_parts, mass, pot = call(
        tile_kernel,
        [(ADS_HERE, USERS_HERE), (NROW, 1, USERS_HERE), (1, USERS_HERE), (1, ADS_HERE)],
        y.reshape(1), z.reshape(1), *messages, ads, weight, pot_parts, fallback, log_demand,
        scalars=2,
    )
    row_parts = lax.all_to_all(row_parts, row_axes, 0, 0, tiled=True)
    row_pot, col_parts = call(
        first_column_kernel,
        [(1, USERS_HERE), (NZ, 1, ADS_HERE)],
        tile, row_parts, mass, pot,
    )
    col_parts = lax.all_to_all(col_parts, "z", 0, 0, tiled=True)
    pot, row_parts = call(
        second_row_kernel,
        [(1, ADS_HERE), (NROW, 1, USERS_HERE)],
        tile, col_parts, row_pot, pot, fallback, log_demand,
    )
    row_parts = lax.all_to_all(row_parts, row_axes, 0, 0, tiled=True)
    users, col_parts = call(
        second_column_kernel,
        [(1, UBS), (NZ, 1, ADS_HERE)],
        mine.reshape(1), tile, row_parts, row_pot, mass, pot,
        scalars=1,
    )
    col_parts = lax.all_to_all(col_parts, "z", 0, 0, tiled=True)
    (last,) = call(
        last_kernel, [(1, SHARD)],
        z.reshape(1), col_parts, pot, fallback, log_demand,
        scalars=1,
    )
    return users.reshape(UBS), last.reshape(SHARD)


def solution(mesh):
    fine = Mesh(mesh.devices.reshape(NZ, NY, NC, NX), ("z", "y", "c", "x"))
    user = ("z", "y", "c")
    in_specs = (
        P(user, None),
        P(user),
        P(user),
        P("x", None),
        P("x"),
        P("x"),
        P("x"),
        P(("x",) + user),
        P(user, "x", None),
        P(user, "x"),
    )
    out_specs = (P(user), P(("x",) + user))
    return jax.shard_map(
        on_device, mesh=fine, in_specs=in_specs, out_specs=out_specs, check_vma=False
    )
```

```python
import functools
import math

import jax
import jax.numpy as jnp
from jax import lax
from jax.experimental import pallas as pl
from jax.experimental.pallas import tpu as pltpu
from jax.sharding import Mesh
from jax.sharding import PartitionSpec as P

ADS_IN_PART = 1024
AB_J = 4
KMAX = 4
UBS = 256
NZ, NY, NC, NX = 16, 4, 2, 4
NS = NY * NC
NROW = NS * NX
ADS_J = 4096
SHARD = 32
USERS_HERE = NS * UBS
ADS_HERE = NZ * SHARD
PART_HERE = ADS_HERE // AB_J
ROWS = UBS + 8

regularizer_epsilon = 0.1
very_low = -1e30
LOG2E = math.log2(math.e)
TO_BITS = LOG2E / regularizer_epsilon
FROM_BITS = regularizer_epsilon / LOG2E
POT_MESSAGE = 2048
WEIGHT = TO_BITS / math.sqrt(128)
COL_SHIFT = 64.0
ROW_SHIFT = 100.0

VMEM_LIMIT = 40 * 1024 * 1024


def as_columns(row):
    return jnp.broadcast_to(row, (128, row.shape[1])).T


def message_kernel(
    eligible, counts, embedding, scale, mass, pot, ad_scale, out, pot_out, ad_scale_out,
    eligible_here, counts_here, embedding_here, mass_here, pot_here, sems,
):
    pairs = [
        (pot, pot_here),
        (eligible, eligible_here),
        (counts, counts_here),
        (mass, mass_here),
        (scale, out.at[pl.ds(UBS, 2), :]),
        (embedding, embedding_here),
        (ad_scale, ad_scale_out),
    ]
    copies = [pltpu.make_async_copy(src, dst, sems.at[i]) for i, (src, dst) in enumerate(pairs)]
    for copy in copies:
        copy.start()
    pot_out[...] = jnp.zeros((NZ, 1, POT_MESSAGE), jnp.float32)
    copies[0].wait()
    pot_out[:, :, :SHARD] = jnp.broadcast_to(pot_here[...][None], (NZ, 1, SHARD))
    copies[1].wait()
    copies[2].wait()
    for q in range(AB_J):
        bias = jnp.float32(very_low)
        for k in range(KMAX):
            hit = jnp.logical_and(k < counts_here[0, 0], eligible_here[0, 0, k] == q)
            bias = jnp.where(hit, jnp.float32(0.0), bias)
        out[UBS + 4 + q : UBS + 5 + q, :] = jnp.full((1, 128), bias, jnp.float32)
    copies[3].wait()
    out[UBS + 2 : UBS + 4, :] = jnp.log2(mass_here[...])
    copies[4].wait()
    copies[5].wait()
    out[:UBS, :] = embedding_here[...].astype(jnp.float32)
    copies[6].wait()


def of_here(array, mine):
    rows = array[pl.ds(lax.shift_right_logical(mine, 2), NZ, stride=2), :]
    turn = lax.rem(128 - lax.rem(mine, 4) * SHARD, 128)
    rows = pltpu.roll(rows, turn, 1)
    return jnp.concatenate([rows[z : z + 1, :SHARD] for z in range(NZ)], axis=1)


def tile_kernel(
    mine, place, msg0, msg1, msg2, msg3, ads, ad_scale, pot_parts, tile, row_lse, log_mass, pot
):
    del place
    weight = as_columns(of_here(ad_scale, mine[0]) * WEIGHT)
    pots = jnp.concatenate(
        [pot_parts[PLANES[0].index(z), :, :SHARD] for z in range(NZ)], axis=1
    ) * TO_BITS
    pot[...] = pots
    pots = as_columns(pots)
    for back, msg in enumerate((msg0, msg1, msg2, msg3)):
        first = lax.rem(lax.shift_right_logical(mine[0], 1) + (NY - back), NY) * NC

        def block(c, carry, msg=msg, first=first):
            users = msg[c, :UBS, :].astype(jnp.bfloat16)
            scale = jnp.concatenate(
                [msg[c, UBS : UBS + 1, :], msg[c, UBS + 1 : UBS + 2, :]], axis=1
            )
            at = pl.ds(pl.multiple_of((first + c) * UBS, UBS), UBS)
            log_mass[:, at] = jnp.concatenate(
                [msg[c, UBS + 2 : UBS + 3, :], msg[c, UBS + 3 : UBS + 4, :]], axis=1
            )
            peaks, totals = [], []
            for q in range(AB_J):
                rows = slice(q * PART_HERE, (q + 1) * PART_HERE)
                product = lax.dot_general(
                    ads[rows, :], users, (((1,), (1,)), ((), ())),
                    preferred_element_type=jnp.float32,
                )
                bias = msg[c, UBS + 4 + q : UBS + 5 + q, :]
                bias = jnp.concatenate([bias, bias], axis=1)
                wide = jnp.concatenate([weight[rows], weight[rows]], axis=1)
                values = product * wide * scale + bias
                tile[rows, at] = values
                values = values + jnp.concatenate([pots[rows], pots[rows]], axis=1)
                peak = jnp.max(values, axis=0, keepdims=True)
                peaks.append(peak)
                totals.append(jnp.sum(jnp.exp2(values - peak), axis=0, keepdims=True))
            peak = functools.reduce(jnp.maximum, peaks)
            total = sum(t * jnp.exp2(p - peak) for p, t in zip(peaks, totals))
            lse = peak + jnp.log2(total)
            row_lse[:, :, at] = jnp.broadcast_to(lse[None], (NROW, 1, UBS))
            return carry

        lax.fori_loop(0, NC, block, 0)


def column_sums(tile, row_pot, pots):
    sums = []
    for q in range(AB_J):
        rows = slice(q * PART_HERE, (q + 1) * PART_HERE)
        total = jnp.zeros((PART_HERE, 128), jnp.float32)
        for t in range(USERS_HERE // 128):
            lanes = slice(t * 128, (t + 1) * 128)
            total = total + jnp.exp2(tile[rows, lanes] + row_pot[:, lanes] + pots[rows])
        sums.append(jnp.sum(total.T, axis=0, keepdims=True))
    return jnp.concatenate(sums, axis=1)


def first_column_kernel(tile, parts, mass, pot, row_pot_out, col_out):
    peak = jnp.max(parts[...], axis=0)
    total = jnp.sum(jnp.exp2(parts[...] - peak[None]), axis=0)
    row_pot = mass[...] - (peak + jnp.log2(total))
    row_pot_out[...] = row_pot
    sums = column_sums(tile, row_pot + COL_SHIFT, as_columns(pot[...]))
    col_out[...] = jnp.broadcast_to(sums[None], (NZ, 1, ADS_HERE))


def column_update(log_sum, fallback, log_demand):
    peak = jnp.maximum(log_sum, fallback)
    return log_demand - (peak + jnp.log2(jnp.exp2(log_sum - peak) + jnp.exp2(fallback - peak)))


def second_row_kernel(
    mine, tile, parts, row_pot, pot, penalty, demand, pot_out, row_out, fallback, log_demand
):
    fallback[...] = of_here(penalty, mine[0]) * -TO_BITS
    log_demand[...] = jnp.log2(of_here(demand, mine[0]))
    sums = jnp.sum(parts[...], axis=0)
    new_pot = column_update(
        jnp.log2(sums) - COL_SHIFT - pot[...], fallback[...], log_demand[...]
    )
    pot_out[...] = new_pot
    pots = as_columns(new_pot)
    for t in range(USERS_HERE // 128):
        lanes = slice(t * 128, (t + 1) * 128)
        shift = row_pot[:, lanes] + ROW_SHIFT
        total = jnp.zeros((8, 128), jnp.float32)
        for q in range(AB_J):
            rows = slice(q * PART_HERE, (q + 1) * PART_HERE)
            terms = jnp.exp2(tile[rows, lanes] + shift + pots[rows])
            total = total + jnp.sum(terms.reshape(PART_HERE // 8, 8, 128), axis=0)
        total = jnp.sum(total, axis=0, keepdims=True)
        row_out[:, :, lanes] = jnp.broadcast_to(total[None], (NROW, 1, 128))


def second_column_kernel(own, tile, parts, row_pot, mass, pot, user_out, col_out):
    sums = jnp.sum(parts[...], axis=0)
    new = row_pot[...] + (mass[...] + ROW_SHIFT - jnp.log2(sums))
    sums = column_sums(tile, new, as_columns(pot[...]))
    col_out[...] = jnp.broadcast_to(sums[None], (NZ, 1, ADS_HERE))
    picked = jnp.zeros((1, UBS), jnp.float32)
    for s in range(NS):
        picked = jnp.where(own[0] == s, new[:, s * UBS : (s + 1) * UBS], picked)
    user_out[...] = picked * FROM_BITS


def last_kernel(own, parts, pot, fallback, log_demand, out):
    sums = jnp.sum(parts[...], axis=0)
    new = column_update(jnp.log2(sums) - pot[...], fallback[...], log_demand[...]) * FROM_BITS
    new = jnp.broadcast_to(new, (8, ADS_HERE))
    turned = pltpu.roll(new, lax.rem(ADS_HERE - own[0] * SHARD, ADS_HERE), 1)
    out[...] = turned[:1, :SHARD]


def call(kernel, out_shape, *operands, scalars=0):
    vmem = pl.BlockSpec(memory_space=pltpu.VMEM)
    smem = pl.BlockSpec(memory_space=pltpu.SMEM)
    return pl.pallas_call(
        kernel,
        out_shape=[jax.ShapeDtypeStruct(s, jnp.float32) for s in out_shape],
        in_specs=[smem] * scalars + [vmem] * (len(operands) - scalars),
        out_specs=[vmem] * len(out_shape),
        compiler_params=pltpu.CompilerParams(vmem_limit_bytes=VMEM_LIMIT),
    )(*operands)


FIRST_Z = NZ // 2
PLANES = [[(FIRST_Z + i) % NZ for i in range(NZ)]]
ROW_GROUP = [
    [
        ((NY // 2 + i) % NY * NC + c) * NX + (NX // 2 + j) % NX
        for i in range(NY)
        for c in range(NC)
        for j in range(NX)
    ]
]


def over_planes(value):
    return lax.all_to_all(value, "z", 0, 0, tiled=True, axis_index_groups=PLANES)


def over_rows(value):
    return lax.all_to_all(
        value, ("y", "c", "x"), 0, 0, tiled=True, axis_index_groups=ROW_GROUP
    )


def on_device(
    user_embedding,
    user_scale,
    user_mass,
    ad_embedding,
    ad_scale,
    listing_view_demand,
    listing_unplaced_penalty,
    campaign_dual_vector_initial,
    eligible,
    counts,
):
    y, z = lax.axis_index("y"), lax.axis_index("z")
    mine = (y * NC + lax.axis_index("c")).reshape(1)
    place = z.reshape(1)

    message, pot_parts, ad_scale = pl.pallas_call(
        message_kernel,
        out_shape=[
            jax.ShapeDtypeStruct((ROWS, 128), jnp.float32),
            jax.ShapeDtypeStruct((NZ, 1, POT_MESSAGE), jnp.float32),
            jax.ShapeDtypeStruct((ADS_J // 128, 128), jnp.float32),
        ],
        in_specs=[pl.BlockSpec(memory_space=pltpu.HBM)] * 7,
        out_specs=[pl.BlockSpec(memory_space=pltpu.VMEM)] * 3,
        scratch_shapes=[
            pltpu.SMEM((1, 1, KMAX), jnp.int32),
            pltpu.SMEM((1, 1), jnp.int32),
            pltpu.VMEM((UBS, 128), jnp.bfloat16),
            pltpu.VMEM((2, 128), jnp.float32),
            pltpu.VMEM((1, SHARD), jnp.float32),
            pltpu.SemaphoreType.DMA((7,)),
        ],
    )(
        eligible, counts, user_embedding, user_scale.reshape(2, 128), user_mass.reshape(2, 128),
        campaign_dual_vector_initial.reshape(1, SHARD), ad_scale.reshape(ADS_J // 128, 128),
    )
    pot_parts = over_planes(pot_parts)
    pair = lax.all_gather(message, "c")
    messages = [pair] + [
        lax.ppermute(pair, "y", [(i, (i + d) % NY) for i in range(NY)]) for d in range(1, NY)
    ]
    ads = lax.dynamic_index_in_dim(
        ad_embedding.reshape(NZ, NS, SHARD, -1), mine[0], 1, keepdims=False
    ).reshape(ADS_HERE, -1)
    demand = listing_view_demand.reshape(ADS_J // 128, 128)
    penalty = listing_unplaced_penalty.reshape(ADS_J // 128, 128)

    tile, row_parts, mass, pot = call(
        tile_kernel,
        [(ADS_HERE, USERS_HERE), (NROW, 1, USERS_HERE), (1, USERS_HERE), (1, ADS_HERE)],
        mine, place, *messages, ads, ad_scale, pot_parts,
        scalars=2,
    )
    row_pot, col_parts = call(
        first_column_kernel,
        [(1, USERS_HERE), (NZ, 1, ADS_HERE)],
        tile, over_rows(row_parts), mass, pot,
    )
    pot, row_parts, fallback, log_demand = call(
        second_row_kernel,
        [(1, ADS_HERE), (NROW, 1, USERS_HERE), (1, ADS_HERE), (1, ADS_HERE)],
        mine, tile, over_planes(col_parts), row_pot, pot, penalty, demand,
        scalars=1,
    )
    users, col_parts = call(
        second_column_kernel,
        [(1, UBS), (NZ, 1, ADS_HERE)],
        mine, tile, over_rows(row_parts), row_pot, mass, pot,
        scalars=1,
    )
    (last,) = call(
        last_kernel, [(1, SHARD)],
        place, over_planes(col_parts), pot, fallback, log_demand,
        scalars=1,
    )
    return users.reshape(UBS), last.reshape(SHARD)


def solution(mesh):
    fine = Mesh(mesh.devices.reshape(NZ, NY, NC, NX), ("z", "y", "c", "x"))
    user = ("z", "y", "c")
    in_specs = (
        P(user, None),
        P(user),
        P(user),
        P("x", None),
        P("x"),
        P("x"),
        P("x"),
        P(("x",) + user),
        P(user, "x", None),
        P(user, "x"),
    )
    out_specs = (P(user), P(("x",) + user))
    return jax.shard_map(
        on_device, mesh=fine, in_specs=in_specs, out_specs=out_specs, check_vma=False
    )
```

```python
import functools
import math

import jax
import jax.numpy as jnp
from jax import lax
from jax.experimental import pallas as pl
from jax.experimental.pallas import tpu as pltpu
from jax.sharding import Mesh
from jax.sharding import PartitionSpec as P

ADS_IN_PART = 1024
AB_J = 4
KMAX = 4
UBS = 256
NZ, NY, NC, NX = 16, 4, 2, 4
NS = NY * NC
NROW = NS * NX
ADS_J = 4096
SHARD = 32
USERS_HERE = NS * UBS
ADS_HERE = NZ * SHARD
PART_HERE = ADS_HERE // AB_J
ROWS = UBS + 8

regularizer_epsilon = 0.1
very_low = -1e30
LOG2E = math.log2(math.e)
TO_BITS = LOG2E / regularizer_epsilon
FROM_BITS = regularizer_epsilon / LOG2E
POT_MESSAGE = 32
WEIGHT = TO_BITS / math.sqrt(128)
COL_SHIFT = 64.0
ROW_SHIFT = 100.0

VMEM_LIMIT = 40 * 1024 * 1024


def as_columns(row):
    return jnp.broadcast_to(row, (128, row.shape[1])).T


def message_kernel(
    eligible, counts, embedding, scale, mass, pot, ad_scale, out, pot_out, ad_scale_out,
    eligible_here, counts_here, embedding_here, mass_here, pot_here, sems,
):
    pairs = [
        (pot, pot_here),
        (eligible, eligible_here),
        (counts, counts_here),
        (mass, mass_here),
        (scale, out.at[pl.ds(UBS, 2), :]),
        (embedding, embedding_here),
        (ad_scale, ad_scale_out),
    ]
    copies = [pltpu.make_async_copy(src, dst, sems.at[i]) for i, (src, dst) in enumerate(pairs)]
    for copy in copies:
        copy.start()
    pot_out[...] = jnp.zeros((NZ, 1, POT_MESSAGE), jnp.float32)
    copies[0].wait()
    pot_out[:, :, :SHARD] = jnp.broadcast_to(pot_here[...][None], (NZ, 1, SHARD))
    copies[1].wait()
    copies[2].wait()
    for q in range(AB_J):
        bias = jnp.float32(very_low)
        for k in range(KMAX):
            hit = jnp.logical_and(k < counts_here[0, 0], eligible_here[0, 0, k] == q)
            bias = jnp.where(hit, jnp.float32(0.0), bias)
        out[UBS + 4 + q : UBS + 5 + q, :] = jnp.full((1, 128), bias, jnp.float32)
    copies[3].wait()
    out[UBS + 2 : UBS + 4, :] = jnp.log2(mass_here[...])
    copies[4].wait()
    copies[5].wait()
    out[:UBS, :] = embedding_here[...].astype(jnp.float32)
    copies[6].wait()


def of_here(array, mine):
    rows = array[pl.ds(lax.shift_right_logical(mine, 2), NZ, stride=2), :]
    turn = lax.rem(128 - lax.rem(mine, 4) * SHARD, 128)
    rows = pltpu.roll(rows, turn, 1)
    return jnp.concatenate([rows[z : z + 1, :SHARD] for z in range(NZ)], axis=1)


def tile_kernel(
    mine, place, msg0, msg1, msg2, msg3, ads, ad_scale, pot_parts, tile, row_lse, log_mass, pot
):
    del place
    weight = as_columns(of_here(ad_scale, mine[0]) * WEIGHT)
    pots = jnp.concatenate(
        [pot_parts[PLANES[0].index(z), :, :SHARD] for z in range(NZ)], axis=1
    ) * TO_BITS
    pot[...] = pots
    pots = as_columns(pots)
    for back, msg in enumerate((msg0, msg1, msg2, msg3)):
        first = lax.rem(lax.shift_right_logical(mine[0], 1) + (NY - back), NY) * NC

        def block(c, carry, msg=msg, first=first):
            users = msg[c, :UBS, :].astype(jnp.bfloat16)
            scale = jnp.concatenate(
                [msg[c, UBS : UBS + 1, :], msg[c, UBS + 1 : UBS + 2, :]], axis=1
            )
            at = pl.ds(pl.multiple_of((first + c) * UBS, UBS), UBS)
            log_mass[:, at] = jnp.concatenate(
                [msg[c, UBS + 2 : UBS + 3, :], msg[c, UBS + 3 : UBS + 4, :]], axis=1
            )
            peaks, totals = [], []
            for q in range(AB_J):
                rows = slice(q * PART_HERE, (q + 1) * PART_HERE)
                product = lax.dot_general(
                    ads[rows, :], users, (((1,), (1,)), ((), ())),
                    preferred_element_type=jnp.float32,
                )
                bias = msg[c, UBS + 4 + q : UBS + 5 + q, :]
                bias = jnp.concatenate([bias, bias], axis=1)
                wide = jnp.concatenate([weight[rows], weight[rows]], axis=1)
                values = product * wide * scale + bias
                tile[rows, at] = values
                values = values + jnp.concatenate([pots[rows], pots[rows]], axis=1)
                peak = jnp.max(values, axis=0, keepdims=True)
                peaks.append(peak)
                totals.append(jnp.sum(jnp.exp2(values - peak), axis=0, keepdims=True))
            peak = functools.reduce(jnp.maximum, peaks)
            total = sum(t * jnp.exp2(p - peak) for p, t in zip(peaks, totals))
            lse = peak + jnp.log2(total)
            row_lse[:, :, at] = jnp.broadcast_to(lse[None], (NROW, 1, UBS))
            return carry

        lax.fori_loop(0, NC, block, 0)


def column_sums(tile, row_pot, pots):
    sums = []
    for q in range(AB_J):
        rows = slice(q * PART_HERE, (q + 1) * PART_HERE)
        total = jnp.zeros((PART_HERE, 128), jnp.float32)
        for t in range(USERS_HERE // 128):
            lanes = slice(t * 128, (t + 1) * 128)
            total = total + jnp.exp2(tile[rows, lanes] + row_pot[:, lanes] + pots[rows])
        sums.append(jnp.sum(total.T, axis=0, keepdims=True))
    return jnp.concatenate(sums, axis=1)


def first_column_kernel(tile, parts, mass, pot, row_pot_out, col_out):
    peak = jnp.max(parts[...], axis=0)
    total = jnp.sum(jnp.exp2(parts[...] - peak[None]), axis=0)
    row_pot = mass[...] - (peak + jnp.log2(total))
    row_pot_out[...] = row_pot
    sums = column_sums(tile, row_pot + COL_SHIFT, as_columns(pot[...]))
    col_out[...] = jnp.broadcast_to(sums[None], (NZ, 1, ADS_HERE))


def column_update(log_sum, fallback, log_demand):
    peak = jnp.maximum(log_sum, fallback)
    return log_demand - (peak + jnp.log2(jnp.exp2(log_sum - peak) + jnp.exp2(fallback - peak)))


def second_row_kernel(
    mine, tile, parts, row_pot, pot, penalty, demand, pot_out, row_out, fallback, log_demand
):
    fallback[...] = of_here(penalty, mine[0]) * -TO_BITS
    log_demand[...] = jnp.log2(of_here(demand, mine[0]))
    sums = jnp.sum(parts[...], axis=0)
    new_pot = column_update(
        jnp.log2(sums) - COL_SHIFT - pot[...], fallback[...], log_demand[...]
    )
    pot_out[...] = new_pot
    pots = as_columns(new_pot)
    for t in range(USERS_HERE // 128):
        lanes = slice(t * 128, (t + 1) * 128)
        shift = row_pot[:, lanes] + ROW_SHIFT
        total = jnp.zeros((8, 128), jnp.float32)
        for q in range(AB_J):
            rows = slice(q * PART_HERE, (q + 1) * PART_HERE)
            terms = jnp.exp2(tile[rows, lanes] + shift + pots[rows])
            total = total + jnp.sum(terms.reshape(PART_HERE // 8, 8, 128), axis=0)
        total = jnp.sum(total, axis=0, keepdims=True)
        row_out[:, :, lanes] = jnp.broadcast_to(total[None], (NROW, 1, 128))


def second_column_kernel(own, tile, parts, row_pot, mass, pot, user_out, col_out):
    sums = jnp.sum(parts[...], axis=0)
    new = row_pot[...] + (mass[...] + ROW_SHIFT - jnp.log2(sums))
    sums = column_sums(tile, new, as_columns(pot[...]))
    col_out[...] = jnp.broadcast_to(sums[None], (NZ, 1, ADS_HERE))
    picked = jnp.zeros((1, UBS), jnp.float32)
    for s in range(NS):
        picked = jnp.where(own[0] == s, new[:, s * UBS : (s + 1) * UBS], picked)
    user_out[...] = picked * FROM_BITS


def last_kernel(own, parts, pot, fallback, log_demand, out):
    sums = jnp.sum(parts[...], axis=0)
    new = column_update(jnp.log2(sums) - pot[...], fallback[...], log_demand[...]) * FROM_BITS
    new = jnp.broadcast_to(new, (8, ADS_HERE))
    turned = pltpu.roll(new, lax.rem(ADS_HERE - own[0] * SHARD, ADS_HERE), 1)
    out[...] = turned[:1, :SHARD]


def call(kernel, out_shape, *operands, scalars=0):
    vmem = pl.BlockSpec(memory_space=pltpu.VMEM)
    smem = pl.BlockSpec(memory_space=pltpu.SMEM)
    return pl.pallas_call(
        kernel,
        out_shape=[jax.ShapeDtypeStruct(s, jnp.float32) for s in out_shape],
        in_specs=[smem] * scalars + [vmem] * (len(operands) - scalars),
        out_specs=[vmem] * len(out_shape),
        compiler_params=pltpu.CompilerParams(vmem_limit_bytes=VMEM_LIMIT),
    )(*operands)


FIRST_Z = NZ // 2
PLANES = [[(FIRST_Z + i) % NZ for i in range(NZ)]]
ROW_GROUP = [
    [
        ((NY // 2 + i) % NY * NC + c) * NX + (NX // 2 + j) % NX
        for i in range(NY)
        for c in range(NC)
        for j in range(NX)
    ]
]


def over_planes(value):
    return lax.all_to_all(value, "z", 0, 0, tiled=True, axis_index_groups=PLANES)


def over_rows(value):
    return lax.all_to_all(
        value, ("y", "c", "x"), 0, 0, tiled=True, axis_index_groups=ROW_GROUP
    )


def on_device(
    user_embedding,
    user_scale,
    user_mass,
    ad_embedding,
    ad_scale,
    listing_view_demand,
    listing_unplaced_penalty,
    campaign_dual_vector_initial,
    eligible,
    counts,
):
    y, z = lax.axis_index("y"), lax.axis_index("z")
    mine = (y * NC + lax.axis_index("c")).reshape(1)
    place = z.reshape(1)

    message, pot_parts, ad_scale = pl.pallas_call(
        message_kernel,
        out_shape=[
            jax.ShapeDtypeStruct((ROWS, 128), jnp.float32),
            jax.ShapeDtypeStruct((NZ, 1, POT_MESSAGE), jnp.float32),
            jax.ShapeDtypeStruct((ADS_J // 128, 128), jnp.float32),
        ],
        in_specs=[pl.BlockSpec(memory_space=pltpu.HBM)] * 7,
        out_specs=[pl.BlockSpec(memory_space=pltpu.VMEM)] * 3,
        scratch_shapes=[
            pltpu.SMEM((1, 1, KMAX), jnp.int32),
            pltpu.SMEM((1, 1), jnp.int32),
            pltpu.VMEM((UBS, 128), jnp.bfloat16),
            pltpu.VMEM((2, 128), jnp.float32),
            pltpu.VMEM((1, SHARD), jnp.float32),
            pltpu.SemaphoreType.DMA((7,)),
        ],
    )(
        eligible, counts, user_embedding, user_scale.reshape(2, 128), user_mass.reshape(2, 128),
        campaign_dual_vector_initial.reshape(1, SHARD), ad_scale.reshape(ADS_J // 128, 128),
    )
    pot_parts = over_planes(pot_parts)
    pair = lax.all_gather(message, "c")
    messages = [pair] + [
        lax.ppermute(pair, "y", [(i, (i + d) % NY) for i in range(NY)]) for d in range(1, NY)
    ]
    ads = lax.dynamic_index_in_dim(
        ad_embedding.reshape(NZ, NS, SHARD, -1), mine[0], 1, keepdims=False
    ).reshape(ADS_HERE, -1)
    demand = listing_view_demand.reshape(ADS_J // 128, 128)
    penalty = listing_unplaced_penalty.reshape(ADS_J // 128, 128)

    tile, row_parts, mass, pot = call(
        tile_kernel,
        [(ADS_HERE, USERS_HERE), (NROW, 1, USERS_HERE), (1, USERS_HERE), (1, ADS_HERE)],
        mine, place, *messages, ads, ad_scale, pot_parts,
        scalars=2,
    )
    row_pot, col_parts = call(
        first_column_kernel,
        [(1, USERS_HERE), (NZ, 1, ADS_HERE)],
        tile, over_rows(row_parts), mass, pot,
    )
    pot, row_parts, fallback, log_demand = call(
        second_row_kernel,
        [(1, ADS_HERE), (NROW, 1, USERS_HERE), (1, ADS_HERE), (1, ADS_HERE)],
        mine, tile, over_planes(col_parts), row_pot, pot, penalty, demand,
        scalars=1,
    )
    users, col_parts = call(
        second_column_kernel,
        [(1, UBS), (NZ, 1, ADS_HERE)],
        mine, tile, over_rows(row_parts), row_pot, mass, pot,
        scalars=1,
    )
    (last,) = call(
        last_kernel, [(1, SHARD)],
        place, over_planes(col_parts), pot, fallback, log_demand,
        scalars=1,
    )
    return users.reshape(UBS), last.reshape(SHARD)


def solution(mesh):
    fine = Mesh(mesh.devices.reshape(NZ, NY, NC, NX), ("z", "y", "c", "x"))
    user = ("z", "y", "c")
    in_specs = (
        P(user, None),
        P(user),
        P(user),
        P("x", None),
        P("x"),
        P("x"),
        P("x"),
        P(("x",) + user),
        P(user, "x", None),
        P(user, "x"),
    )
    out_specs = (P(user), P(("x",) + user))
    return jax.shard_map(
        on_device, mesh=fine, in_specs=in_specs, out_specs=out_specs, check_vma=False
    )
```

```python
import functools
import math

import jax
import jax.numpy as jnp
from jax import lax
from jax.experimental import pallas as pl
from jax.experimental.pallas import tpu as pltpu
from jax.sharding import Mesh
from jax.sharding import PartitionSpec as P

ADS_IN_PART = 1024
AB_J = 4
KMAX = 4
UBS = 256
NZ, NY, NC, NX = 16, 4, 2, 4
NS = NY * NC
NROW = NS * NX
ADS_J = 4096
SHARD = 32
USERS_HERE = NS * UBS
ADS_HERE = NZ * SHARD
PART_HERE = ADS_HERE // AB_J
ROWS = UBS + 8

regularizer_epsilon = 0.1
very_low = -1e30
LOG2E = math.log2(math.e)
TO_BITS = LOG2E / regularizer_epsilon
FROM_BITS = regularizer_epsilon / LOG2E
WEIGHT = TO_BITS / math.sqrt(128)
COL_SHIFT = 64.0
ROW_SHIFT = 100.0

VMEM_LIMIT = 40 * 1024 * 1024


def as_columns(row):
    return jnp.broadcast_to(row, (128, row.shape[1])).T


def message_kernel(
    eligible, counts, embedding, scale, mass, pot, out, pot_out,
    eligible_here, counts_here, embedding_here, mass_here, pot_here, sems,
):
    pairs = [
        (pot, pot_here),
        (eligible, eligible_here),
        (counts, counts_here),
        (mass, mass_here),
        (scale, out.at[pl.ds(UBS, 2), :]),
        (embedding, embedding_here),
    ]
    copies = [pltpu.make_async_copy(src, dst, sems.at[i]) for i, (src, dst) in enumerate(pairs)]
    for copy in copies:
        copy.start()
    copies[0].wait()
    pot_out[...] = jnp.broadcast_to(pot_here[...][None], (NZ, 1, SHARD))
    copies[1].wait()
    copies[2].wait()
    for q in range(AB_J):
        bias = jnp.float32(very_low)
        for k in range(KMAX):
            hit = jnp.logical_and(k < counts_here[0, 0], eligible_here[0, 0, k] == q)
            bias = jnp.where(hit, jnp.float32(0.0), bias)
        out[UBS + 4 + q : UBS + 5 + q, :] = jnp.full((1, 128), bias, jnp.float32)
    copies[3].wait()
    out[UBS + 2 : UBS + 4, :] = jnp.log2(mass_here[...])
    copies[4].wait()
    copies[5].wait()
    out[:UBS, :] = embedding_here[...].astype(jnp.float32)


def of_here(array, mine):
    rows = array[pl.ds(lax.shift_right_logical(mine, 2), NZ, stride=2), :]
    turn = lax.rem(128 - lax.rem(mine, 4) * SHARD, 128)
    rows = pltpu.roll(rows, turn, 1)
    return jnp.concatenate([rows[z : z + 1, :SHARD] for z in range(NZ)], axis=1)


def tile_kernel(
    mine, place, msg0, msg1, msg2, msg3, ads, ad_weight, pot_parts, tile, row_lse, log_mass, pot
):
    del place
    weight = as_columns(of_here(ad_weight, mine[0]))
    pots = jnp.concatenate(
        [pot_parts[PLANES[0].index(z)] for z in range(NZ)], axis=1
    ) * TO_BITS
    pot[...] = pots
    pots = as_columns(pots)
    for back, msg in enumerate((msg0, msg1, msg2, msg3)):
        first = lax.rem(lax.shift_right_logical(mine[0], 1) + (NY - back), NY) * NC

        for c in range(NC):
            users = msg[c, :UBS, :].astype(jnp.bfloat16)
            scale = jnp.concatenate(
                [msg[c, UBS : UBS + 1, :], msg[c, UBS + 1 : UBS + 2, :]], axis=1
            )
            at = pl.ds(pl.multiple_of((first + c) * UBS, UBS), UBS)
            log_mass[:, at] = jnp.concatenate(
                [msg[c, UBS + 2 : UBS + 3, :], msg[c, UBS + 3 : UBS + 4, :]], axis=1
            )
            peaks, totals = [], []
            for q in range(AB_J):
                rows = slice(q * PART_HERE, (q + 1) * PART_HERE)
                product = lax.dot_general(
                    ads[rows, :], users, (((1,), (1,)), ((), ())),
                    preferred_element_type=jnp.float32,
                )
                bias = msg[c, UBS + 4 + q : UBS + 5 + q, :]
                bias = jnp.concatenate([bias, bias], axis=1)
                wide = jnp.concatenate([weight[rows], weight[rows]], axis=1)
                values = product * wide * scale + bias
                tile[rows, at] = values
                values = values + jnp.concatenate([pots[rows], pots[rows]], axis=1)
                peak = jnp.max(values, axis=0, keepdims=True)
                peaks.append(peak)
                totals.append(jnp.sum(jnp.exp2(values - peak), axis=0, keepdims=True))
            peak = functools.reduce(jnp.maximum, peaks)
            total = sum(t * jnp.exp2(p - peak) for p, t in zip(peaks, totals))
            lse = peak + jnp.log2(total)
            row_lse[:, :, at] = jnp.broadcast_to(lse[None], (NROW, 1, UBS))


def column_sums(tile, row_pot, pots):
    sums = []
    for q in range(AB_J):
        rows = slice(q * PART_HERE, (q + 1) * PART_HERE)
        total = jnp.zeros((PART_HERE, 128), jnp.float32)
        for t in range(USERS_HERE // 128):
            lanes = slice(t * 128, (t + 1) * 128)
            total = total + jnp.exp2(tile[rows, lanes] + row_pot[:, lanes] + pots[rows])
        sums.append(jnp.sum(total.T, axis=0, keepdims=True))
    return jnp.concatenate(sums, axis=1)


def first_column_kernel(tile, parts, mass, pot, row_pot_out, col_out):
    peak = jnp.max(parts[...], axis=0)
    total = jnp.sum(jnp.exp2(parts[...] - peak[None]), axis=0)
    row_pot = mass[...] - (peak + jnp.log2(total))
    row_pot_out[...] = row_pot
    sums = column_sums(tile, row_pot + COL_SHIFT, as_columns(pot[...]))
    col_out[...] = jnp.broadcast_to(sums[None], (NZ, 1, ADS_HERE))


def column_update(log_sum, fallback, log_demand):
    peak = jnp.maximum(log_sum, fallback)
    return log_demand - (peak + jnp.log2(jnp.exp2(log_sum - peak) + jnp.exp2(fallback - peak)))


def second_row_kernel(
    mine, tile, parts, row_pot, pot, penalty, demand, pot_out, row_out, fallback, log_demand
):
    fallback[...] = of_here(penalty, mine[0]) * -TO_BITS
    log_demand[...] = jnp.log2(of_here(demand, mine[0]))
    sums = jnp.sum(parts[...], axis=0)
    new_pot = column_update(
        jnp.log2(sums) - COL_SHIFT - pot[...], fallback[...], log_demand[...]
    )
    pot_out[...] = new_pot
    pots = as_columns(new_pot)
    for t in range(USERS_HERE // 128):
        lanes = slice(t * 128, (t + 1) * 128)
        shift = row_pot[:, lanes] + ROW_SHIFT
        total = jnp.zeros((8, 128), jnp.float32)
        for q in range(AB_J):
            rows = slice(q * PART_HERE, (q + 1) * PART_HERE)
            terms = jnp.exp2(tile[rows, lanes] + shift + pots[rows])
            total = total + jnp.sum(terms.reshape(PART_HERE // 8, 8, 128), axis=0)
        total = jnp.sum(total, axis=0, keepdims=True)
        row_out[:, :, lanes] = jnp.broadcast_to(total[None], (NROW, 1, 128))


def second_column_kernel(own, tile, parts, row_pot, mass, pot, user_out, col_out):
    sums = jnp.sum(parts[...], axis=0)
    new = row_pot[...] + (mass[...] + ROW_SHIFT - jnp.log2(sums))
    sums = column_sums(tile, new, as_columns(pot[...]))
    col_out[...] = jnp.broadcast_to(sums[None], (NZ, 1, ADS_HERE))
    picked = jnp.zeros((1, UBS), jnp.float32)
    for s in range(NS):
        picked = jnp.where(own[0] == s, new[:, s * UBS : (s + 1) * UBS], picked)
    user_out[...] = picked * FROM_BITS


def last_kernel(own, parts, pot, fallback, log_demand, out):
    sums = jnp.sum(parts[...], axis=0)
    new = column_update(jnp.log2(sums) - pot[...], fallback[...], log_demand[...]) * FROM_BITS
    new = jnp.broadcast_to(new, (8, ADS_HERE))
    turned = pltpu.roll(new, lax.rem(ADS_HERE - own[0] * SHARD, ADS_HERE), 1)
    out[...] = turned[:1, :SHARD]


def call(kernel, out_shape, *operands, scalars=0):
    vmem = pl.BlockSpec(memory_space=pltpu.VMEM)
    smem = pl.BlockSpec(memory_space=pltpu.SMEM)
    return pl.pallas_call(
        kernel,
        out_shape=[jax.ShapeDtypeStruct(s, jnp.float32) for s in out_shape],
        in_specs=[smem] * scalars + [vmem] * (len(operands) - scalars),
        out_specs=[vmem] * len(out_shape),
        compiler_params=pltpu.CompilerParams(vmem_limit_bytes=VMEM_LIMIT),
    )(*operands)


FIRST_Z = NZ // 2
PLANES = [[(FIRST_Z + i) % NZ for i in range(NZ)]]
ROW_GROUP = [
    [
        ((NY // 2 + i) % NY * NC + c) * NX + (NX // 2 + j) % NX
        for i in range(NY)
        for c in range(NC)
        for j in range(NX)
    ]
]


def over_planes(value):
    return lax.all_to_all(value, "z", 0, 0, tiled=True, axis_index_groups=PLANES)


def over_rows(value):
    return lax.all_to_all(
        value, ("y", "c", "x"), 0, 0, tiled=True, axis_index_groups=ROW_GROUP
    )


def on_device(
    user_embedding,
    user_scale,
    user_mass,
    ad_embedding,
    ad_scale,
    listing_view_demand,
    listing_unplaced_penalty,
    campaign_dual_vector_initial,
    eligible,
    counts,
):
    y, z = lax.axis_index("y"), lax.axis_index("z")
    mine = (y * NC + lax.axis_index("c")).reshape(1)
    place = z.reshape(1)

    message, pot_parts = pl.pallas_call(
        message_kernel,
        out_shape=[
            jax.ShapeDtypeStruct((ROWS, 128), jnp.float32),
            jax.ShapeDtypeStruct((NZ, 1, SHARD), jnp.float32),
        ],
        in_specs=[pl.BlockSpec(memory_space=pltpu.HBM)] * 6,
        out_specs=[pl.BlockSpec(memory_space=pltpu.VMEM)] * 2,
        scratch_shapes=[
            pltpu.SMEM((1, 1, KMAX), jnp.int32),
            pltpu.SMEM((1, 1), jnp.int32),
            pltpu.VMEM((UBS, 128), jnp.bfloat16),
            pltpu.VMEM((2, 128), jnp.float32),
            pltpu.VMEM((1, SHARD), jnp.float32),
            pltpu.SemaphoreType.DMA((6,)),
        ],
    )(
        eligible, counts, user_embedding, user_scale.reshape(2, 128), user_mass.reshape(2, 128),
        campaign_dual_vector_initial.reshape(1, SHARD),
    )
    pot_parts = over_planes(pot_parts)
    pair = lax.all_gather(message, "c")
    behind = {
        d: lax.ppermute(pair, "y", [(i, (i + d) % NY) for i in range(NY)]) for d in (1, 2, 3)
    }
    messages = [pair, behind[1], behind[2], behind[3]]
    ads = lax.dynamic_index_in_dim(
        ad_embedding.reshape(NZ, NS, SHARD, -1), mine[0], 1, keepdims=False
    ).reshape(ADS_HERE, -1)
    ad_weight = ad_scale.reshape(ADS_J // 128, 128) * WEIGHT
    demand = listing_view_demand.reshape(ADS_J // 128, 128)
    penalty = listing_unplaced_penalty.reshape(ADS_J // 128, 128)

    tile, row_parts, mass, pot = call(
        tile_kernel,
        [(ADS_HERE, USERS_HERE), (NROW, 1, USERS_HERE), (1, USERS_HERE), (1, ADS_HERE)],
        mine, place, *messages, ads, ad_weight, pot_parts,
        scalars=2,
    )
    row_pot, col_parts = call(
        first_column_kernel,
        [(1, USERS_HERE), (NZ, 1, ADS_HERE)],
        tile, over_rows(row_parts), mass, pot,
    )
    pot, row_parts, fallback, log_demand = call(
        second_row_kernel,
        [(1, ADS_HERE), (NROW, 1, USERS_HERE), (1, ADS_HERE), (1, ADS_HERE)],
        mine, tile, over_planes(col_parts), row_pot, pot, penalty, demand,
        scalars=1,
    )
    users, col_parts = call(
        second_column_kernel,
        [(1, UBS), (NZ, 1, ADS_HERE)],
        mine, tile, over_rows(row_parts), row_pot, mass, pot,
        scalars=1,
    )
    (last,) = call(
        last_kernel, [(1, SHARD)],
        place, over_planes(col_parts), pot, fallback, log_demand,
        scalars=1,
    )
    return users.reshape(UBS), last.reshape(SHARD)


def solution(mesh):
    fine = Mesh(mesh.devices.reshape(NZ, NY, NC, NX), ("z", "y", "c", "x"))
    user = ("z", "y", "c")
    in_specs = (
        P(user, None),
        P(user),
        P(user),
        P("x", None),
        P("x"),
        P("x"),
        P("x"),
        P(("x",) + user),
        P(user, "x", None),
        P(user, "x"),
    )
    out_specs = (P(user), P(("x",) + user))
    return jax.shard_map(
        on_device, mesh=fine, in_specs=in_specs, out_specs=out_specs, check_vma=False
    )
```

```python
import functools
import math

import jax
import jax.numpy as jnp
from jax import lax
from jax.experimental import pallas as pl
from jax.experimental.pallas import tpu as pltpu
from jax.sharding import Mesh
from jax.sharding import PartitionSpec as P

ADS_IN_PART = 1024
AB_J = 4
KMAX = 4
UBS = 256
NZ, NY, NC, NX = 16, 4, 2, 4
NS = NY * NC
NROW = NS * NX
ADS_J = 4096
SHARD = 32
USERS_HERE = NS * UBS
ADS_HERE = NZ * SHARD
PART_HERE = ADS_HERE // AB_J
ROWS = UBS + 8 + 32

regularizer_epsilon = 0.1
very_low = -1e30
TO_UNITS = 1.0 / regularizer_epsilon
WEIGHT = TO_UNITS / math.sqrt(128)
COL_SHIFT = 44.0
ROW_SHIFT = 69.0

VMEM_LIMIT = 40 * 1024 * 1024


def as_columns(row):
    return jnp.broadcast_to(row, (128, row.shape[1])).T


def my_block():
    return lax.axis_index("y") * NC + lax.axis_index("c")


def message_kernel(
    eligible, counts, embedding, scale, mass, pot, ad_scale, out, pot_out,
    eligible_here, counts_here, embedding_here, mass_here, pot_here, sems,
):
    pairs = [
        (pot, pot_here),
        (eligible, eligible_here),
        (counts, counts_here),
        (mass, mass_here),
        (scale, out.at[pl.ds(UBS, 2), :]),
        (embedding, embedding_here),
        (ad_scale, out.at[pl.ds(UBS + 8, 32), :]),
    ]
    copies = [pltpu.make_async_copy(src, dst, sems.at[i]) for i, (src, dst) in enumerate(pairs)]
    for copy in copies:
        copy.start()
    copies[0].wait()
    pot_out[...] = jnp.broadcast_to(pot_here[...][None], (NZ, 1, SHARD))
    copies[1].wait()
    copies[2].wait()
    for q in range(AB_J):
        bias = jnp.float32(very_low)
        for k in range(KMAX):
            hit = jnp.logical_and(k < counts_here[0, 0], eligible_here[0, 0, k] == q)
            bias = jnp.where(hit, jnp.float32(0.0), bias)
        out[UBS + 4 + q : UBS + 5 + q, :] = jnp.full((1, 128), bias, jnp.float32)
    copies[3].wait()
    out[UBS + 2 : UBS + 4, :] = jnp.log(mass_here[...])
    copies[4].wait()
    copies[5].wait()
    out[:UBS, :] = embedding_here[...].astype(jnp.float32)
    copies[6].wait()


def of_here(array, mine):
    rows = array[pl.ds(lax.shift_right_logical(mine, 2), NZ, stride=2), :]
    turn = lax.rem(128 - lax.rem(mine, 4) * SHARD, 128)
    rows = pltpu.roll(rows, turn, 1)
    return jnp.concatenate([rows[z : z + 1, :SHARD] for z in range(NZ)], axis=1)


def tile_kernel(
    msg0, msg1, msg2, msg3, ads, pot_parts, tile, row_lse, log_mass, pot, lse_here
):
    mine = my_block()
    weight = as_columns(of_here(msg0.at[lax.rem(mine, NC), pl.ds(UBS + 8, 32), :], mine) * WEIGHT)
    pots = jnp.concatenate(
        [pot_parts[PLANES[0].index(z)] for z in range(NZ)], axis=1
    ) * TO_UNITS
    pot[...] = pots
    pots = as_columns(pots)
    for back, msg in enumerate((msg0, msg1, msg2, msg3)):
        first = lax.rem(lax.shift_right_logical(mine, 1) + (NY - back), NY) * NC

        for c in range(NC):
            users = msg[c, :UBS, :].astype(jnp.bfloat16)
            scale = jnp.concatenate(
                [msg[c, UBS : UBS + 1, :], msg[c, UBS + 1 : UBS + 2, :]], axis=1
            )
            at = pl.ds(pl.multiple_of((first + c) * UBS, UBS), UBS)
            log_mass[pl.ds(first + c, 1), :] = jnp.concatenate(
                [msg[c, UBS + 2 : UBS + 3, :], msg[c, UBS + 3 : UBS + 4, :]], axis=1
            )
            peaks, totals = [], []
            for q in range(AB_J):
                rows = slice(q * PART_HERE, (q + 1) * PART_HERE)
                product = lax.dot_general(
                    ads[rows, :], users, (((1,), (1,)), ((), ())),
                    preferred_element_type=jnp.float32,
                )
                bias = msg[c, UBS + 4 + q : UBS + 5 + q, :]
                bias = jnp.concatenate([bias, bias], axis=1)
                wide = jnp.concatenate([weight[rows], weight[rows]], axis=1)
                values = product * wide * scale + bias
                tile[rows, at] = values
                values = values + jnp.concatenate([pots[rows], pots[rows]], axis=1)
                peak = jnp.max(values, axis=0, keepdims=True)
                peaks.append(peak)
                totals.append(jnp.sum(jnp.exp(values - peak), axis=0, keepdims=True))
            peak = functools.reduce(jnp.maximum, peaks)
            total = sum(t * jnp.exp(p - peak) for p, t in zip(peaks, totals))
            lse = peak + jnp.log(total)
            lse_here[pl.ds(first + c, 1), :] = lse
    row_lse[...] = jnp.broadcast_to(lse_here[...][None], (NROW, NS, UBS))


def row_of(blocks, t):
    half = t % 2 * 128
    return blocks[t // 2 : t // 2 + 1, half : half + 128]


def column_sums(tile, row_pot, pots):
    sums = []
    for q in range(AB_J):
        rows = slice(q * PART_HERE, (q + 1) * PART_HERE)
        total = jnp.zeros((PART_HERE, 128), jnp.float32)
        for t in range(USERS_HERE // 128):
            lanes = slice(t * 128, (t + 1) * 128)
            total = total + jnp.exp(tile[rows, lanes] + row_of(row_pot, t) + pots[rows])
        sums.append(jnp.sum(total.T, axis=0, keepdims=True))
    return jnp.concatenate(sums, axis=1)


def first_column_kernel(tile, parts, mass, pot, row_pot_out, col_out):
    peak = jnp.max(parts[...], axis=0)
    total = jnp.sum(jnp.exp(parts[...] - peak[None]), axis=0)
    row_pot = mass[...] - (peak + jnp.log(total))
    row_pot_out[...] = row_pot
    sums = column_sums(tile, row_pot + COL_SHIFT, as_columns(pot[...]))
    col_out[...] = jnp.broadcast_to(sums[None], (NZ, 1, ADS_HERE))


def column_update(log_sum, fallback, log_demand):
    peak = jnp.maximum(log_sum, fallback)
    return log_demand - (peak + jnp.log(jnp.exp(log_sum - peak) + jnp.exp(fallback - peak)))


def second_row_kernel(
    tile, parts, row_pot, pot, penalty, demand, pot_out, row_out, fallback, log_demand, sums_here
):
    mine = my_block()
    fallback[...] = of_here(penalty, mine) * -TO_UNITS
    log_demand[...] = jnp.log(of_here(demand, mine))
    sums = jnp.sum(parts[...], axis=0)
    new_pot = column_update(
        jnp.log(sums) - COL_SHIFT - pot[...], fallback[...], log_demand[...]
    )
    pot_out[...] = new_pot
    pots = as_columns(new_pot)
    for t in range(USERS_HERE // 128):
        lanes = slice(t * 128, (t + 1) * 128)
        shift = row_of(row_pot, t) + ROW_SHIFT
        total = jnp.zeros((8, 128), jnp.float32)
        for q in range(AB_J):
            rows = slice(q * PART_HERE, (q + 1) * PART_HERE)
            terms = jnp.exp(tile[rows, lanes] + shift + pots[rows])
            total = total + jnp.sum(terms.reshape(PART_HERE // 8, 8, 128), axis=0)
        half = t % 2 * 128
        sums_here[t // 2 : t // 2 + 1, half : half + 128] = jnp.sum(total, axis=0, keepdims=True)
    row_out[...] = jnp.broadcast_to(sums_here[...][None], (NROW, NS, UBS))


def second_column_kernel(tile, parts, row_pot, mass, pot, new_out, col_out):
    sums = jnp.sum(parts[...], axis=0)
    new = row_pot[...] + (mass[...] + ROW_SHIFT - jnp.log(sums))
    new_out[...] = new
    sums = column_sums(tile, new, as_columns(pot[...]))
    col_out[...] = jnp.broadcast_to(sums[None], (NZ, 1, ADS_HERE))


def last_kernel(parts, pot, fallback, log_demand, row_pot, out, user_out):
    user_out[...] = row_pot[pl.ds(my_block(), 1), :] * regularizer_epsilon
    sums = jnp.sum(parts[...], axis=0)
    new = column_update(
        jnp.log(sums) - pot[...], fallback[...], log_demand[...]
    ) * regularizer_epsilon
    new = jnp.broadcast_to(new, (8, ADS_HERE))
    turned = pltpu.roll(new, lax.rem(ADS_HERE - lax.axis_index("z") * SHARD, ADS_HERE), 1)
    out[...] = turned[:1, :SHARD]


def call(kernel, out_shape, *operands, scratch=()):
    vmem = pl.BlockSpec(memory_space=pltpu.VMEM)
    return pl.pallas_call(
        kernel,
        out_shape=[jax.ShapeDtypeStruct(s, jnp.float32) for s in out_shape],
        in_specs=[vmem] * len(operands),
        out_specs=[vmem] * len(out_shape),
        scratch_shapes=[pltpu.VMEM(shape, jnp.float32) for shape in scratch],
        compiler_params=pltpu.CompilerParams(vmem_limit_bytes=VMEM_LIMIT),
    )(*operands)


FIRST_Z = NZ // 2
PLANES = [[8, 15, 6, 13, 4, 11, 2, 9, 0, 7, 14, 5, 12, 3, 10, 1]]
ROW_GROUP = [
    [
        ((NY // 2 + i) % NY * NC + c) * NX + (NX // 2 + j) % NX
        for i in range(NY)
        for c in (1, 0)
        for j in range(NX)
    ]
]


def over_planes(value):
    return lax.all_to_all(value, "z", 0, 0, tiled=True, axis_index_groups=PLANES)


def over_rows(value):
    return lax.all_to_all(
        value, ("y", "c", "x"), 0, 0, tiled=True, axis_index_groups=ROW_GROUP
    )


def on_device(
    user_embedding,
    user_scale,
    user_mass,
    ad_embedding,
    ad_scale,
    listing_view_demand,
    listing_unplaced_penalty,
    campaign_dual_vector_initial,
    eligible,
    counts,
):

    message, pot_parts = pl.pallas_call(
        message_kernel,
        out_shape=[
            jax.ShapeDtypeStruct((ROWS, 128), jnp.float32),
            jax.ShapeDtypeStruct((NZ, 1, SHARD), jnp.float32),
        ],
        in_specs=[pl.BlockSpec(memory_space=pltpu.HBM)] * 7,
        out_specs=[pl.BlockSpec(memory_space=pltpu.VMEM)] * 2,
        scratch_shapes=[
            pltpu.SMEM((1, 1, KMAX), jnp.int32),
            pltpu.SMEM((1, 1), jnp.int32),
            pltpu.VMEM((UBS, 128), jnp.bfloat16),
            pltpu.VMEM((2, 128), jnp.float32),
            pltpu.VMEM((1, SHARD), jnp.float32),
            pltpu.SemaphoreType.DMA((7,)),
        ],
    )(
        eligible, counts, user_embedding, user_scale.reshape(2, 128), user_mass.reshape(2, 128),
        campaign_dual_vector_initial.reshape(1, SHARD), ad_scale.reshape(ADS_J // 128, 128),
    )
    ads = lax.dynamic_index_in_dim(
        ad_embedding.reshape(NZ, NS, SHARD, -1), my_block(), 1, keepdims=False
    ).reshape(ADS_HERE, -1)
    ads, pot_parts = lax.optimization_barrier((ads, pot_parts))
    pot_parts = over_planes(pot_parts)
    pair = lax.all_gather(message, "c")
    behind = {
        d: lax.ppermute(pair, "y", [(i, (i + d) % NY) for i in range(NY)]) for d in (1, 2, 3)
    }
    messages = [pair, behind[1], behind[2], behind[3]]
    demand = listing_view_demand.reshape(ADS_J // 128, 128)
    penalty = listing_unplaced_penalty.reshape(ADS_J // 128, 128)

    tile, row_parts, mass, pot = call(
        tile_kernel,
        [(ADS_HERE, USERS_HERE), (NROW, NS, UBS), (NS, UBS), (1, ADS_HERE)],
        *messages, ads, pot_parts,
        scratch=[(NS, UBS)],
    )
    row_pot, col_parts = call(
        first_column_kernel,
        [(NS, UBS), (NZ, 1, ADS_HERE)],
        tile, over_rows(row_parts), mass, pot,
    )
    pot, row_parts, fallback, log_demand = call(
        second_row_kernel,
        [(1, ADS_HERE), (NROW, NS, UBS), (1, ADS_HERE), (1, ADS_HERE)],
        tile, over_planes(col_parts), row_pot, pot, penalty, demand,
        scratch=[(NS, UBS)],
    )
    new_row_pot, col_parts = call(
        second_column_kernel,
        [(NS, UBS), (NZ, 1, ADS_HERE)],
        tile, over_rows(row_parts), row_pot, mass, pot,
    )
    last, users = call(
        last_kernel,
        [(1, SHARD), (1, UBS)],
        over_planes(col_parts), pot, fallback, log_demand, new_row_pot,
    )
    return users.reshape(UBS), last.reshape(SHARD)


def solution(mesh):
    fine = Mesh(mesh.devices.reshape(NZ, NY, NC, NX), ("z", "y", "c", "x"))
    user = ("z", "y", "c")
    in_specs = (
        P(user, None),
        P(user),
        P(user),
        P("x", None),
        P("x"),
        P("x"),
        P("x"),
        P(("x",) + user),
        P(user, "x", None),
        P(user, "x"),
    )
    out_specs = (P(user), P(("x",) + user))
    return jax.shard_map(
        on_device, mesh=fine, in_specs=in_specs, out_specs=out_specs, check_vma=False
    )
```

```python
import functools
import math

import jax
import jax.numpy as jnp
from jax import lax
from jax.experimental import pallas as pl
from jax.experimental.pallas import tpu as pltpu
from jax.sharding import Mesh
from jax.sharding import PartitionSpec as P

ADS_IN_PART = 1024
AB_J = 4
KMAX = 4
UBS = 256
NZ, NY, NC, NX = 16, 4, 2, 4
NS = NY * NC
NROW = NS * NX
ADS_J = 4096
SHARD = 32
USERS_HERE = NS * UBS
ADS_HERE = NZ * SHARD
PART_HERE = ADS_HERE // AB_J
ROWS = UBS + 8

regularizer_epsilon = 0.1
very_low = -1e30
TO_UNITS = 1.0 / regularizer_epsilon
WEIGHT = TO_UNITS / math.sqrt(128)
COL_SHIFT = 44.0
ROW_SHIFT = 69.0

VMEM_LIMIT = 40 * 1024 * 1024


def as_columns(row):
    return jnp.broadcast_to(row, (128, row.shape[1])).T


def my_block():
    return lax.axis_index("y") * NC + lax.axis_index("c")


def message_kernel(
    eligible, counts, embedding, scale, mass, pot, out, pot_out,
    eligible_here, counts_here, embedding_here, mass_here, pot_here, sems,
):
    pairs = [
        (pot, pot_here),
        (eligible, eligible_here),
        (counts, counts_here),
        (mass, mass_here),
        (scale, out.at[pl.ds(UBS, 2), :]),
        (embedding, embedding_here),
    ]
    copies = [pltpu.make_async_copy(src, dst, sems.at[i]) for i, (src, dst) in enumerate(pairs)]
    for copy in copies:
        copy.start()
    copies[0].wait()
    pot_out[...] = jnp.broadcast_to(pot_here[...][None], (NZ, 1, SHARD))
    copies[1].wait()
    copies[2].wait()
    for q in range(AB_J):
        bias = jnp.float32(very_low)
        for k in range(KMAX):
            hit = jnp.logical_and(k < counts_here[0, 0], eligible_here[0, 0, k] == q)
            bias = jnp.where(hit, jnp.float32(0.0), bias)
        out[UBS + 4 + q : UBS + 5 + q, :] = jnp.full((1, 128), bias, jnp.float32)
    copies[3].wait()
    out[UBS + 2 : UBS + 4, :] = jnp.log(mass_here[...])
    copies[4].wait()
    copies[5].wait()
    out[:UBS, :] = embedding_here[...].astype(jnp.float32)


def of_here(array, mine):
    rows = array[pl.ds(lax.shift_right_logical(mine, 2), NZ, stride=2), :]
    turn = lax.rem(128 - lax.rem(mine, 4) * SHARD, 128)
    rows = pltpu.roll(rows, turn, 1)
    return jnp.concatenate([rows[z : z + 1, :SHARD] for z in range(NZ)], axis=1)


def tile_kernel(
    msg0, msg1, msg3, msg2, ads, ad_weight, pot_parts, tile, row_lse, log_mass, pot, lse_here
):
    mine = my_block()
    weight = as_columns(of_here(ad_weight, mine))
    pots = jnp.concatenate(
        [pot_parts[PLANES[0].index(z)] for z in range(NZ)], axis=1
    ) * TO_UNITS
    pot[...] = pots
    pots = as_columns(pots)
    for back, msg in ((0, msg0), (1, msg1), (3, msg3), (2, msg2)):
        first = lax.bitwise_xor(lax.shift_right_logical(mine, 1), back) * NC

        for c in range(NC):
            users = msg[c, :UBS, :].astype(jnp.bfloat16)
            scale = jnp.concatenate(
                [msg[c, UBS : UBS + 1, :], msg[c, UBS + 1 : UBS + 2, :]], axis=1
            )
            at = pl.ds(pl.multiple_of((first + c) * UBS, UBS), UBS)
            log_mass[pl.ds(first + c, 1), :] = jnp.concatenate(
                [msg[c, UBS + 2 : UBS + 3, :], msg[c, UBS + 3 : UBS + 4, :]], axis=1
            )
            peaks, totals = [], []
            for q in range(AB_J):
                rows = slice(q * PART_HERE, (q + 1) * PART_HERE)
                product = lax.dot_general(
                    ads[rows, :], users, (((1,), (1,)), ((), ())),
                    preferred_element_type=jnp.float32,
                )
                bias = msg[c, UBS + 4 + q : UBS + 5 + q, :]
                bias = jnp.concatenate([bias, bias], axis=1)
                wide = jnp.concatenate([weight[rows], weight[rows]], axis=1)
                values = product * wide * scale + bias
                tile[rows, at] = values
                values = values + jnp.concatenate([pots[rows], pots[rows]], axis=1)
                peak = jnp.max(values, axis=0, keepdims=True)
                peaks.append(peak)
                totals.append(jnp.sum(jnp.exp(values - peak), axis=0, keepdims=True))
            peak = functools.reduce(jnp.maximum, peaks)
            total = sum(t * jnp.exp(p - peak) for p, t in zip(peaks, totals))
            lse = peak + jnp.log(total)
            lse_here[pl.ds(first + c, 1), :] = lse
    row_lse[...] = jnp.broadcast_to(lse_here[...][None], (NROW, NS, UBS))


def row_of(blocks, t):
    half = t % 2 * 128
    return blocks[t // 2 : t // 2 + 1, half : half + 128]


def column_sums(tile, row_pot, pots):
    sums = []
    for q in range(AB_J):
        rows = slice(q * PART_HERE, (q + 1) * PART_HERE)
        total = jnp.zeros((PART_HERE, 128), jnp.float32)
        for t in range(USERS_HERE // 128):
            lanes = slice(t * 128, (t + 1) * 128)
            total = total + jnp.exp(tile[rows, lanes] + row_of(row_pot, t) + pots[rows])
        sums.append(jnp.sum(total.T, axis=0, keepdims=True))
    return jnp.concatenate(sums, axis=1)


def first_column_kernel(tile, parts, mass, pot, row_pot_out, col_out):
    peak = jnp.max(parts[...], axis=0)
    total = jnp.sum(jnp.exp(parts[...] - peak[None]), axis=0)
    row_pot = mass[...] - (peak + jnp.log(total))
    row_pot_out[...] = row_pot
    sums = column_sums(tile, row_pot + COL_SHIFT, as_columns(pot[...]))
    col_out[...] = jnp.broadcast_to(sums[None], (NZ, 1, ADS_HERE))


def column_update(log_sum, fallback, log_demand):
    peak = jnp.maximum(log_sum, fallback)
    return log_demand - (peak + jnp.log(jnp.exp(log_sum - peak) + jnp.exp(fallback - peak)))


def second_row_kernel(
    tile, parts, row_pot, pot, penalty, demand, pot_out, row_out, fallback, log_demand, sums_here
):
    mine = my_block()
    fallback[...] = of_here(penalty, mine) * -TO_UNITS
    log_demand[...] = jnp.log(of_here(demand, mine))
    sums = jnp.sum(parts[...], axis=0)
    new_pot = column_update(
        jnp.log(sums) - COL_SHIFT - pot[...], fallback[...], log_demand[...]
    )
    pot_out[...] = new_pot
    pots = as_columns(new_pot)
    for t in range(USERS_HERE // 128):
        lanes = slice(t * 128, (t + 1) * 128)
        shift = row_of(row_pot, t) + ROW_SHIFT
        total = jnp.zeros((8, 128), jnp.float32)
        for q in range(AB_J):
            rows = slice(q * PART_HERE, (q + 1) * PART_HERE)
            terms = jnp.exp(tile[rows, lanes] + shift + pots[rows])
            total = total + jnp.sum(terms.reshape(PART_HERE // 8, 8, 128), axis=0)
        half = t % 2 * 128
        sums_here[t // 2 : t // 2 + 1, half : half + 128] = jnp.sum(total, axis=0, keepdims=True)
    row_out[...] = jnp.broadcast_to(sums_here[...][None], (NROW, NS, UBS))


def second_column_kernel(tile, parts, row_pot, mass, pot, new_out, col_out):
    sums = jnp.sum(parts[...], axis=0)
    new = row_pot[...] + (mass[...] + ROW_SHIFT - jnp.log(sums))
    new_out[...] = new
    sums = column_sums(tile, new, as_columns(pot[...]))
    col_out[...] = jnp.broadcast_to(sums[None], (NZ, 1, ADS_HERE))


def last_kernel(parts, pot, fallback, log_demand, row_pot, out, user_out):
    user_out[...] = row_pot[pl.ds(my_block(), 1), :] * regularizer_epsilon
    sums = jnp.sum(parts[...], axis=0)
    new = column_update(
        jnp.log(sums) - pot[...], fallback[...], log_demand[...]
    ) * regularizer_epsilon
    new = jnp.broadcast_to(new, (8, ADS_HERE))
    turned = pltpu.roll(new, lax.rem(ADS_HERE - lax.axis_index("z") * SHARD, ADS_HERE), 1)
    out[...] = turned[:1, :SHARD]


def call(kernel, out_shape, *operands, scratch=()):
    vmem = pl.BlockSpec(memory_space=pltpu.VMEM)
    return pl.pallas_call(
        kernel,
        out_shape=[jax.ShapeDtypeStruct(s, jnp.float32) for s in out_shape],
        in_specs=[vmem] * len(operands),
        out_specs=[vmem] * len(out_shape),
        scratch_shapes=[pltpu.VMEM(shape, jnp.float32) for shape in scratch],
        compiler_params=pltpu.CompilerParams(vmem_limit_bytes=VMEM_LIMIT),
    )(*operands)


FIRST_Z = NZ // 2
PLANES = [[8, 15, 6, 13, 4, 11, 2, 9, 0, 7, 14, 5, 12, 3, 10, 1]]
ROW_GROUP = [
    [
        ((NY // 2 + i) % NY * NC + c) * NX + (NX // 2 + j) % NX
        for i in range(NY)
        for c in (1, 0)
        for j in range(NX)
    ]
]


def over_planes(value):
    return lax.all_to_all(value, "z", 0, 0, tiled=True, axis_index_groups=PLANES)


def over_rows(value):
    return lax.all_to_all(
        value, ("y", "c", "x"), 0, 0, tiled=True, axis_index_groups=ROW_GROUP
    )


def on_device(
    user_embedding,
    user_scale,
    user_mass,
    ad_embedding,
    ad_scale,
    listing_view_demand,
    listing_unplaced_penalty,
    campaign_dual_vector_initial,
    eligible,
    counts,
):

    message, pot_parts = pl.pallas_call(
        message_kernel,
        out_shape=[
            jax.ShapeDtypeStruct((ROWS, 128), jnp.float32),
            jax.ShapeDtypeStruct((NZ, 1, SHARD), jnp.float32),
        ],
        in_specs=[pl.BlockSpec(memory_space=pltpu.HBM)] * 6,
        out_specs=[pl.BlockSpec(memory_space=pltpu.VMEM)] * 2,
        scratch_shapes=[
            pltpu.SMEM((1, 1, KMAX), jnp.int32),
            pltpu.SMEM((1, 1), jnp.int32),
            pltpu.VMEM((UBS, 128), jnp.bfloat16),
            pltpu.VMEM((2, 128), jnp.float32),
            pltpu.VMEM((1, SHARD), jnp.float32),
            pltpu.SemaphoreType.DMA((6,)),
        ],
    )(
        eligible, counts, user_embedding, user_scale.reshape(2, 128), user_mass.reshape(2, 128),
        campaign_dual_vector_initial.reshape(1, SHARD),
    )
    ads = lax.dynamic_index_in_dim(
        ad_embedding.reshape(NZ, NS, SHARD, -1), my_block(), 1, keepdims=False
    ).reshape(ADS_HERE, -1)
    pot_parts = over_planes(pot_parts)
    pair = lax.all_gather(message, "c")
    behind = {
        d: lax.ppermute(pair, "y", [(i, i ^ d) for i in range(NY)]) for d in (1, 2, 3)
    }
    messages = [pair, behind[1], behind[3], behind[2]]
    demand = listing_view_demand.reshape(ADS_J // 128, 128)
    penalty = listing_unplaced_penalty.reshape(ADS_J // 128, 128)

    tile, row_parts, mass, pot = call(
        tile_kernel,
        [(ADS_HERE, USERS_HERE), (NROW, NS, UBS), (NS, UBS), (1, ADS_HERE)],
        *messages, ads, ad_scale.reshape(ADS_J // 128, 128) * WEIGHT, pot_parts,
        scratch=[(NS, UBS)],
    )
    row_pot, col_parts = call(
        first_column_kernel,
        [(NS, UBS), (NZ, 1, ADS_HERE)],
        tile, over_rows(row_parts), mass, pot,
    )
    pot, row_parts, fallback, log_demand = call(
        second_row_kernel,
        [(1, ADS_HERE), (NROW, NS, UBS), (1, ADS_HERE), (1, ADS_HERE)],
        tile, over_planes(col_parts), row_pot, pot, penalty, demand,
        scratch=[(NS, UBS)],
    )
    new_row_pot, col_parts = call(
        second_column_kernel,
        [(NS, UBS), (NZ, 1, ADS_HERE)],
        tile, over_rows(row_parts), row_pot, mass, pot,
    )
    last, users = call(
        last_kernel,
        [(1, SHARD), (1, UBS)],
        over_planes(col_parts), pot, fallback, log_demand, new_row_pot,
    )
    return users.reshape(UBS), last.reshape(SHARD)


def solution(mesh):
    fine = Mesh(mesh.devices.reshape(NZ, NY, NC, NX), ("z", "y", "c", "x"))
    user = ("z", "y", "c")
    in_specs = (
        P(user, None),
        P(user),
        P(user),
        P("x", None),
        P("x"),
        P("x"),
        P("x"),
        P(("x",) + user),
        P(user, "x", None),
        P(user, "x"),
    )
    out_specs = (P(user), P(("x",) + user))
    return jax.shard_map(
        on_device, mesh=fine, in_specs=in_specs, out_specs=out_specs, check_vma=False
    )
```

```python
import functools
import math

import jax
import jax.numpy as jnp
from jax import lax
from jax.experimental import pallas as pl
from jax.experimental.pallas import tpu as pltpu
from jax.sharding import Mesh
from jax.sharding import PartitionSpec as P

ADS_IN_PART = 1024
AB_J = 4
KMAX = 4
UBS = 256
NZ, NY, NC, NX = 16, 4, 2, 4
NS = NY * NC
NROW = NS * NX
ADS_J = 4096
SHARD = 32
USERS_HERE = NS * UBS
ADS_HERE = NZ * SHARD
PART_HERE = ADS_HERE // AB_J
ROWS = UBS + 8

regularizer_epsilon = 0.1
very_low = -1e30
TO_UNITS = 1.0 / regularizer_epsilon
WEIGHT = TO_UNITS / math.sqrt(128)
COL_SHIFT = 44.0
ROW_SHIFT = 69.0

VMEM_LIMIT = 40 * 1024 * 1024


def as_columns(row):
    return jnp.broadcast_to(row, (128, row.shape[1])).T


def my_block():
    return lax.axis_index("y") * NC + lax.axis_index("c")


def message_kernel(
    eligible, counts, embedding, scale, mass, pot, out, pot_out,
    eligible_here, counts_here, embedding_here, mass_here, pot_here, sems,
):
    pairs = [
        (pot, pot_here),
        (eligible, eligible_here),
        (counts, counts_here),
        (mass, mass_here),
        (scale, out.at[pl.ds(UBS, 2), :]),
        (embedding, embedding_here),
    ]
    copies = [pltpu.make_async_copy(src, dst, sems.at[i]) for i, (src, dst) in enumerate(pairs)]
    for copy in copies:
        copy.start()
    copies[0].wait()
    row = jnp.concatenate([pot_here[...], jnp.zeros((1, 128 - SHARD), jnp.float32)], axis=1)
    row = pltpu.roll(
        jnp.broadcast_to(row, (8, 128)), lax.rem(lax.axis_index("z"), 4) * SHARD, 1
    )
    pot_out[...] = jnp.broadcast_to(row[:1][None], (NZ, 1, 128))
    copies[1].wait()
    copies[2].wait()
    for q in range(AB_J):
        bias = jnp.float32(very_low)
        for k in range(KMAX):
            hit = jnp.logical_and(k < counts_here[0, 0], eligible_here[0, 0, k] == q)
            bias = jnp.where(hit, jnp.float32(0.0), bias)
        out[UBS + 4 + q : UBS + 5 + q, :] = jnp.full((1, 128), bias, jnp.float32)
    copies[3].wait()
    out[UBS + 2 : UBS + 4, :] = jnp.log(mass_here[...])
    copies[4].wait()
    copies[5].wait()
    out[:UBS, :] = embedding_here[...].astype(jnp.float32)


def of_here(array, mine):
    rows = array[pl.ds(lax.shift_right_logical(mine, 2), NZ, stride=2), :]
    place = lax.broadcasted_iota(jnp.int32, (NZ, 128), 1) // SHARD
    plane = lax.broadcasted_iota(jnp.int32, (NZ, 128), 0) % 4
    placed = jnp.zeros((NZ, 128), jnp.float32)
    for i in range(4):
        turn = lax.rem(128 + i * SHARD - lax.rem(mine, 4) * SHARD, 128)
        here = jnp.logical_and(place == i, plane == i)
        placed = jnp.where(here, pltpu.roll(rows, turn, 1), placed)
    rows = placed
    return jnp.concatenate(
        [jnp.sum(rows[z : z + 4], axis=0, keepdims=True) for z in range(0, NZ, 4)], axis=1
    )


def tile_kernel(
    msg0, msg1, msg3, msg2, ads, ad_weight, pot_parts, tile, row_lse, log_mass, pot, lse_here
):
    mine = my_block()
    weight = as_columns(of_here(ad_weight, mine))
    pots = jnp.concatenate(
        [sum(pot_parts[PLANES[0].index(z + i)] for i in range(4)) for z in range(0, NZ, 4)],
        axis=1,
    ) * TO_UNITS
    pot[...] = pots
    pots = as_columns(pots)
    for back, msg in ((0, msg0), (1, msg1), (3, msg3), (2, msg2)):
        first = lax.bitwise_xor(lax.shift_right_logical(mine, 1), back) * NC

        for c in range(NC):
            users = msg[c, :UBS, :].astype(jnp.bfloat16)
            scale = jnp.concatenate(
                [msg[c, UBS : UBS + 1, :], msg[c, UBS + 1 : UBS + 2, :]], axis=1
            )
            at = pl.ds(pl.multiple_of((first + c) * UBS, UBS), UBS)
            log_mass[pl.ds(first + c, 1), :] = jnp.concatenate(
                [msg[c, UBS + 2 : UBS + 3, :], msg[c, UBS + 3 : UBS + 4, :]], axis=1
            )
            peaks, totals = [], []
            for q in range(AB_J):
                rows = slice(q * PART_HERE, (q + 1) * PART_HERE)
                product = lax.dot_general(
                    ads[rows, :], users, (((1,), (1,)), ((), ())),
                    preferred_element_type=jnp.float32,
                )
                bias = msg[c, UBS + 4 + q : UBS + 5 + q, :]
                bias = jnp.concatenate([bias, bias], axis=1)
                wide = jnp.concatenate([weight[rows], weight[rows]], axis=1)
                values = product * wide * scale + bias
                tile[rows, at] = values
                values = values + jnp.concatenate([pots[rows], pots[rows]], axis=1)
                peak = jnp.max(values, axis=0, keepdims=True)
                peaks.append(peak)
                totals.append(jnp.sum(jnp.exp(values - peak), axis=0, keepdims=True))
            peak = functools.reduce(jnp.maximum, peaks)
            total = sum(t * jnp.exp(p - peak) for p, t in zip(peaks, totals))
            lse = peak + jnp.log(total)
            lse_here[pl.ds(first + c, 1), :] = lse
    row_lse[...] = jnp.broadcast_to(lse_here[...][None], (NROW, NS, UBS))


def row_of(blocks, t):
    half = t % 2 * 128
    return blocks[t // 2 : t // 2 + 1, half : half + 128]


def column_sums(tile, row_pot, pots):
    sums = []
    for q in range(AB_J):
        rows = slice(q * PART_HERE, (q + 1) * PART_HERE)
        total = jnp.zeros((PART_HERE, 128), jnp.float32)
        for t in range(USERS_HERE // 128):
            lanes = slice(t * 128, (t + 1) * 128)
            total = total + jnp.exp(tile[rows, lanes] + row_of(row_pot, t) + pots[rows])
        sums.append(jnp.sum(total.T, axis=0, keepdims=True))
    return jnp.concatenate(sums, axis=1)


def first_column_kernel(tile, parts, mass, pot, row_pot_out, col_out):
    peak = jnp.max(parts[...], axis=0)
    total = jnp.sum(jnp.exp(parts[...] - peak[None]), axis=0)
    row_pot = mass[...] - (peak + jnp.log(total))
    row_pot_out[...] = row_pot
    sums = column_sums(tile, row_pot + COL_SHIFT, as_columns(pot[...]))
    col_out[...] = jnp.broadcast_to(sums[None], (NZ, 1, ADS_HERE))


def column_update(log_sum, fallback, log_demand):
    peak = jnp.maximum(log_sum, fallback)
    return log_demand - (peak + jnp.log(jnp.exp(log_sum - peak) + jnp.exp(fallback - peak)))


def second_row_kernel(
    tile, parts, row_pot, pot, penalty, demand, pot_out, row_out, fallback, log_demand, sums_here
):
    mine = my_block()
    fallback[...] = of_here(penalty, mine) * -TO_UNITS
    log_demand[...] = jnp.log(of_here(demand, mine))
    sums = jnp.sum(parts[...], axis=0)
    new_pot = column_update(
        jnp.log(sums) - COL_SHIFT - pot[...], fallback[...], log_demand[...]
    )
    pot_out[...] = new_pot
    pots = as_columns(new_pot)
    for t in range(USERS_HERE // 128):
        lanes = slice(t * 128, (t + 1) * 128)
        shift = row_of(row_pot, t) + ROW_SHIFT
        total = jnp.zeros((8, 128), jnp.float32)
        for q in range(AB_J):
            rows = slice(q * PART_HERE, (q + 1) * PART_HERE)
            terms = jnp.exp(tile[rows, lanes] + shift + pots[rows])
            total = total + jnp.sum(terms.reshape(PART_HERE // 8, 8, 128), axis=0)
        half = t % 2 * 128
        sums_here[t // 2 : t // 2 + 1, half : half + 128] = jnp.sum(total, axis=0, keepdims=True)
    row_out[...] = jnp.broadcast_to(sums_here[...][None], (NROW, NS, UBS))


def second_column_kernel(tile, parts, row_pot, mass, pot, new_out, col_out):
    sums = jnp.sum(parts[...], axis=0)
    new = row_pot[...] + (mass[...] + ROW_SHIFT - jnp.log(sums))
    new_out[...] = new
    sums = column_sums(tile, new, as_columns(pot[...]))
    col_out[...] = jnp.broadcast_to(sums[None], (NZ, 1, ADS_HERE))


def last_kernel(parts, pot, fallback, log_demand, row_pot, out, user_out):
    user_out[...] = row_pot[pl.ds(my_block(), 1), :] * regularizer_epsilon
    sums = jnp.sum(parts[...], axis=0)
    new = column_update(
        jnp.log(sums) - pot[...], fallback[...], log_demand[...]
    ) * regularizer_epsilon
    new = jnp.broadcast_to(new, (8, ADS_HERE))
    turned = pltpu.roll(new, lax.rem(ADS_HERE - lax.axis_index("z") * SHARD, ADS_HERE), 1)
    out[...] = turned[:1, :SHARD]


def call(kernel, out_shape, *operands, scratch=()):
    vmem = pl.BlockSpec(memory_space=pltpu.VMEM)
    return pl.pallas_call(
        kernel,
        out_shape=[jax.ShapeDtypeStruct(s, jnp.float32) for s in out_shape],
        in_specs=[vmem] * len(operands),
        out_specs=[vmem] * len(out_shape),
        scratch_shapes=[pltpu.VMEM(shape, jnp.float32) for shape in scratch],
        compiler_params=pltpu.CompilerParams(vmem_limit_bytes=VMEM_LIMIT),
    )(*operands)


FIRST_Z = NZ // 2
PLANES = [[8, 15, 6, 13, 4, 11, 2, 9, 0, 7, 14, 5, 12, 3, 10, 1]]
ROW_GROUP = [
    [
        ((NY // 2 + i) % NY * NC + c) * NX + (NX // 2 + j) % NX
        for i in range(NY)
        for c in (1, 0)
        for j in range(NX)
    ]
]


def over_planes(value):
    return lax.all_to_all(value, "z", 0, 0, tiled=True, axis_index_groups=PLANES)


def over_rows(value):
    return lax.all_to_all(
        value, ("y", "c", "x"), 0, 0, tiled=True, axis_index_groups=ROW_GROUP
    )


def on_device(
    user_embedding,
    user_scale,
    user_mass,
    ad_embedding,
    ad_scale,
    listing_view_demand,
    listing_unplaced_penalty,
    campaign_dual_vector_initial,
    eligible,
    counts,
):

    message, pot_parts = pl.pallas_call(
        message_kernel,
        out_shape=[
            jax.ShapeDtypeStruct((ROWS, 128), jnp.float32),
            jax.ShapeDtypeStruct((NZ, 1, 128), jnp.float32),
        ],
        in_specs=[pl.BlockSpec(memory_space=pltpu.HBM)] * 6,
        out_specs=[pl.BlockSpec(memory_space=pltpu.VMEM)] * 2,
        scratch_shapes=[
            pltpu.SMEM((1, 1, KMAX), jnp.int32),
            pltpu.SMEM((1, 1), jnp.int32),
            pltpu.VMEM((UBS, 128), jnp.bfloat16),
            pltpu.VMEM((2, 128), jnp.float32),
            pltpu.VMEM((1, SHARD), jnp.float32),
            pltpu.SemaphoreType.DMA((6,)),
        ],
    )(
        eligible, counts, user_embedding, user_scale.reshape(2, 128), user_mass.reshape(2, 128),
        campaign_dual_vector_initial.reshape(1, SHARD),
    )
    ads = lax.dynamic_index_in_dim(
        ad_embedding.reshape(NZ, NS, SHARD, -1), my_block(), 1, keepdims=False
    ).reshape(ADS_HERE, -1)
    pot_parts = over_planes(pot_parts)
    pair = lax.all_gather(message, "c")
    behind = {
        d: lax.ppermute(pair, "y", [(i, i ^ d) for i in range(NY)]) for d in (1, 2, 3)
    }
    messages = [pair, behind[1], behind[3], behind[2]]
    demand = listing_view_demand.reshape(ADS_J // 128, 128)
    penalty = listing_unplaced_penalty.reshape(ADS_J // 128, 128)

    tile, row_parts, mass, pot = call(
        tile_kernel,
        [(ADS_HERE, USERS_HERE), (NROW, NS, UBS), (NS, UBS), (1, ADS_HERE)],
        *messages, ads, ad_scale.reshape(ADS_J // 128, 128) * WEIGHT, pot_parts,
        scratch=[(NS, UBS)],
    )
    row_pot, col_parts = call(
        first_column_kernel,
        [(NS, UBS), (NZ, 1, ADS_HERE)],
        tile, over_rows(row_parts), mass, pot,
    )
    pot, row_parts, fallback, log_demand = call(
        second_row_kernel,
        [(1, ADS_HERE), (NROW, NS, UBS), (1, ADS_HERE), (1, ADS_HERE)],
        tile, over_planes(col_parts), row_pot, pot, penalty, demand,
        scratch=[(NS, UBS)],
    )
    new_row_pot, col_parts = call(
        second_column_kernel,
        [(NS, UBS), (NZ, 1, ADS_HERE)],
        tile, over_rows(row_parts), row_pot, mass, pot,
    )
    last, users = call(
        last_kernel,
        [(1, SHARD), (1, UBS)],
        over_planes(col_parts), pot, fallback, log_demand, new_row_pot,
    )
    return users.reshape(UBS), last.reshape(SHARD)


def solution(mesh):
    fine = Mesh(mesh.devices.reshape(NZ, NY, NC, NX), ("z", "y", "c", "x"))
    user = ("z", "y", "c")
    in_specs = (
        P(user, None),
        P(user),
        P(user),
        P("x", None),
        P("x"),
        P("x"),
        P("x"),
        P(("x",) + user),
        P(user, "x", None),
        P(user, "x"),
    )
    out_specs = (P(user), P(("x",) + user))
    return jax.shard_map(
        on_device, mesh=fine, in_specs=in_specs, out_specs=out_specs, check_vma=False
    )
```

```python
import functools
import math

import jax
import jax.numpy as jnp
from jax import lax
from jax.experimental import pallas as pl
from jax.experimental.pallas import tpu as pltpu
from jax.sharding import Mesh
from jax.sharding import PartitionSpec as P

ADS_IN_PART = 1024
AB_J = 4
KMAX = 4
UBS = 256
NZ, NY, NC, NX = 16, 4, 2, 4
NS = NY * NC
NROW = NS * NX
ADS_J = 4096
SHARD = 32
USERS_HERE = NS * UBS
ADS_HERE = NZ * SHARD
PART_HERE = ADS_HERE // AB_J
ROWS = UBS + 8

regularizer_epsilon = 0.1
very_low = -1e30
TO_UNITS = 1.0 / regularizer_epsilon
WEIGHT = TO_UNITS / math.sqrt(128)
COL_SHIFT = 44.0
ROW_SHIFT = 69.0

VMEM_LIMIT = 40 * 1024 * 1024


def as_columns(row):
    return jnp.broadcast_to(row, (128, row.shape[1])).T


def my_block():
    return lax.axis_index("y") * NC + lax.axis_index("c")


def message_kernel(
    eligible, counts, embedding, scale, mass, pot, out, pot_out,
    eligible_here, counts_here, embedding_here, mass_here, pot_here, sems,
):
    pairs = [
        (pot, pot_here),
        (eligible, eligible_here),
        (counts, counts_here),
        (mass, mass_here),
        (scale, out.at[pl.ds(UBS, 2), :]),
        (embedding, embedding_here),
    ]
    copies = [pltpu.make_async_copy(src, dst, sems.at[i]) for i, (src, dst) in enumerate(pairs)]
    for copy in copies:
        copy.start()
    copies[0].wait()
    row = jnp.concatenate([pot_here[...], jnp.zeros((1, 128 - SHARD), jnp.float32)], axis=1)
    row = pltpu.roll(
        jnp.broadcast_to(row, (8, 128)), lax.rem(lax.axis_index("z"), 4) * SHARD, 1
    )
    pot_out[...] = jnp.broadcast_to(row[:1][None], (NZ, 1, 128))
    copies[1].wait()
    copies[2].wait()
    for q in range(AB_J):
        bias = jnp.float32(very_low)
        for k in range(KMAX):
            hit = jnp.logical_and(k < counts_here[0, 0], eligible_here[0, 0, k] == q)
            bias = jnp.where(hit, jnp.float32(0.0), bias)
        out[UBS + 4 + q : UBS + 5 + q, :] = jnp.full((1, 128), bias, jnp.float32)
    copies[3].wait()
    out[UBS + 2 : UBS + 4, :] = jnp.log(mass_here[...])
    copies[4].wait()
    copies[5].wait()
    out[:UBS, :] = embedding_here[...].astype(jnp.float32)


def of_here(array, mine):
    rows = array[pl.ds(lax.shift_right_logical(mine, 2), NZ, stride=2), :]
    place = lax.broadcasted_iota(jnp.int32, (NZ, 128), 1) // SHARD
    plane = lax.broadcasted_iota(jnp.int32, (NZ, 128), 0) % 4
    placed = jnp.zeros((NZ, 128), jnp.float32)
    for i in range(4):
        turn = lax.rem(128 + i * SHARD - lax.rem(mine, 4) * SHARD, 128)
        here = jnp.logical_and(place == i, plane == i)
        placed = jnp.where(here, pltpu.roll(rows, turn, 1), placed)
    rows = placed
    return jnp.concatenate(
        [jnp.sum(rows[z : z + 4], axis=0, keepdims=True) for z in range(0, NZ, 4)], axis=1
    )


def tile_kernel(
    msg0, msg1, msg3, msg2, ads, ad_weight, pot_parts, tile, row_lse, log_mass, pot, lse_here
):
    mine = my_block()
    weight = as_columns(of_here(ad_weight, mine))
    pots = jnp.concatenate(
        [sum(pot_parts[PLANES[0].index(z + i)] for i in range(4)) for z in range(0, NZ, 4)],
        axis=1,
    ) * TO_UNITS
    pot[...] = pots
    pots = as_columns(pots)
    for back, msg in ((0, msg0), (1, msg1), (3, msg3), (2, msg2)):
        first = lax.bitwise_xor(lax.shift_right_logical(mine, 1), back) * NC

        for c in range(NC):
            users = msg[c, :UBS, :].astype(jnp.bfloat16)
            scale = jnp.concatenate(
                [msg[c, UBS : UBS + 1, :], msg[c, UBS + 1 : UBS + 2, :]], axis=1
            )
            at = pl.ds(pl.multiple_of((first + c) * UBS, UBS), UBS)
            log_mass[pl.ds(first + c, 1), :] = jnp.concatenate(
                [msg[c, UBS + 2 : UBS + 3, :], msg[c, UBS + 3 : UBS + 4, :]], axis=1
            )
            peaks, totals = [], []
            for q in range(AB_J):
                rows = slice(q * PART_HERE, (q + 1) * PART_HERE)
                if q % 2 == 0:
                    products = lax.dot_general(
                        ads[q * PART_HERE : q * PART_HERE + 256, :], users, (((1,), (1,)), ((), ())),
                        preferred_element_type=jnp.float32,
                    )
                product = products[q % 2 * PART_HERE : (q % 2 + 1) * PART_HERE]
                bias = msg[c, UBS + 4 + q : UBS + 5 + q, :]
                bias = jnp.concatenate([bias, bias], axis=1)
                wide = jnp.concatenate([weight[rows], weight[rows]], axis=1)
                values = product * wide * scale + bias
                tile[rows, at] = values
                values = values + jnp.concatenate([pots[rows], pots[rows]], axis=1)
                peak = jnp.max(values, axis=0, keepdims=True)
                peaks.append(peak)
                totals.append(jnp.sum(jnp.exp(values - peak), axis=0, keepdims=True))
            peak = functools.reduce(jnp.maximum, peaks)
            total = sum(t * jnp.exp(p - peak) for p, t in zip(peaks, totals))
            lse = peak + jnp.log(total)
            lse_here[pl.ds(first + c, 1), :] = lse
    row_lse[...] = jnp.broadcast_to(lse_here[...][None], (NROW, NS, UBS))


def row_of(blocks, t):
    half = t % 2 * 128
    return blocks[t // 2 : t // 2 + 1, half : half + 128]


def column_sums(tile, row_pot, pots):
    sums = []
    for q in range(AB_J):
        rows = slice(q * PART_HERE, (q + 1) * PART_HERE)
        total = jnp.zeros((PART_HERE, 128), jnp.float32)
        for t in range(USERS_HERE // 128):
            lanes = slice(t * 128, (t + 1) * 128)
            total = total + jnp.exp(tile[rows, lanes] + row_of(row_pot, t) + pots[rows])
        sums.append(jnp.sum(total.T, axis=0, keepdims=True))
    return jnp.concatenate(sums, axis=1)


def first_column_kernel(tile, parts, mass, pot, row_pot_out, col_out):
    peak = jnp.max(parts[...], axis=0)
    total = jnp.sum(jnp.exp(parts[...] - peak[None]), axis=0)
    row_pot = mass[...] - (peak + jnp.log(total))
    row_pot_out[...] = row_pot
    sums = column_sums(tile, row_pot + COL_SHIFT, as_columns(pot[...]))
    col_out[...] = jnp.broadcast_to(sums[None], (NZ, 1, ADS_HERE))


def column_update(log_sum, fallback, log_demand):
    peak = jnp.maximum(log_sum, fallback)
    return log_demand - (peak + jnp.log(jnp.exp(log_sum - peak) + jnp.exp(fallback - peak)))


def second_row_kernel(
    tile, parts, row_pot, pot, penalty, demand, pot_out, row_out, fallback, log_demand, sums_here
):
    mine = my_block()
    fallback[...] = of_here(penalty, mine) * -TO_UNITS
    log_demand[...] = jnp.log(of_here(demand, mine))
    sums = jnp.sum(parts[...], axis=0)
    new_pot = column_update(
        jnp.log(sums) - COL_SHIFT - pot[...], fallback[...], log_demand[...]
    )
    pot_out[...] = new_pot
    pots = as_columns(new_pot)
    for t in range(USERS_HERE // 128):
        lanes = slice(t * 128, (t + 1) * 128)
        shift = row_of(row_pot, t) + ROW_SHIFT
        total = jnp.zeros((8, 128), jnp.float32)
        for q in range(AB_J):
            rows = slice(q * PART_HERE, (q + 1) * PART_HERE)
            terms = jnp.exp(tile[rows, lanes] + shift + pots[rows])
            total = total + jnp.sum(terms.reshape(PART_HERE // 8, 8, 128), axis=0)
        half = t % 2 * 128
        sums_here[t // 2 : t // 2 + 1, half : half + 128] = jnp.sum(total, axis=0, keepdims=True)
    row_out[...] = jnp.broadcast_to(sums_here[...][None], (NROW, NS, UBS))


def second_column_kernel(tile, parts, row_pot, mass, pot, new_out, col_out):
    sums = jnp.sum(parts[...], axis=0)
    new = row_pot[...] + (mass[...] + ROW_SHIFT - jnp.log(sums))
    new_out[...] = new
    sums = column_sums(tile, new, as_columns(pot[...]))
    col_out[...] = jnp.broadcast_to(sums[None], (NZ, 1, ADS_HERE))


def last_kernel(parts, pot, fallback, log_demand, row_pot, out, user_out):
    user_out[...] = row_pot[pl.ds(my_block(), 1), :] * regularizer_epsilon
    sums = jnp.sum(parts[...], axis=0)
    new = column_update(
        jnp.log(sums) - pot[...], fallback[...], log_demand[...]
    ) * regularizer_epsilon
    new = jnp.broadcast_to(new, (8, ADS_HERE))
    turned = pltpu.roll(new, lax.rem(ADS_HERE - lax.axis_index("z") * SHARD, ADS_HERE), 1)
    out[...] = turned[:1, :SHARD]


def call(kernel, out_shape, *operands, scratch=()):
    vmem = pl.BlockSpec(memory_space=pltpu.VMEM)
    return pl.pallas_call(
        kernel,
        out_shape=[jax.ShapeDtypeStruct(s, jnp.float32) for s in out_shape],
        in_specs=[vmem] * len(operands),
        out_specs=[vmem] * len(out_shape),
        scratch_shapes=[pltpu.VMEM(shape, jnp.float32) for shape in scratch],
        compiler_params=pltpu.CompilerParams(vmem_limit_bytes=VMEM_LIMIT),
    )(*operands)


FIRST_Z = NZ // 2
PLANES = [[8, 15, 6, 13, 4, 11, 2, 9, 0, 7, 14, 5, 12, 3, 10, 1]]
ROW_GROUP = [
    [
        ((NY // 2 + i) % NY * NC + c) * NX + (NX // 2 + j) % NX
        for i in range(NY)
        for c in (1, 0)
        for j in range(NX)
    ]
]


def over_planes(value):
    return lax.all_to_all(value, "z", 0, 0, tiled=True, axis_index_groups=PLANES)


def over_rows(value):
    return lax.all_to_all(
        value, ("y", "c", "x"), 0, 0, tiled=True, axis_index_groups=ROW_GROUP
    )


def on_device(
    user_embedding,
    user_scale,
    user_mass,
    ad_embedding,
    ad_scale,
    listing_view_demand,
    listing_unplaced_penalty,
    campaign_dual_vector_initial,
    eligible,
    counts,
):

    message, pot_parts = pl.pallas_call(
        message_kernel,
        out_shape=[
            jax.ShapeDtypeStruct((ROWS, 128), jnp.float32),
            jax.ShapeDtypeStruct((NZ, 1, 128), jnp.float32),
        ],
        in_specs=[pl.BlockSpec(memory_space=pltpu.HBM)] * 6,
        out_specs=[pl.BlockSpec(memory_space=pltpu.VMEM)] * 2,
        scratch_shapes=[
            pltpu.SMEM((1, 1, KMAX), jnp.int32),
            pltpu.SMEM((1, 1), jnp.int32),
            pltpu.VMEM((UBS, 128), jnp.bfloat16),
            pltpu.VMEM((2, 128), jnp.float32),
            pltpu.VMEM((1, SHARD), jnp.float32),
            pltpu.SemaphoreType.DMA((6,)),
        ],
    )(
        eligible, counts, user_embedding, user_scale.reshape(2, 128), user_mass.reshape(2, 128),
        campaign_dual_vector_initial.reshape(1, SHARD),
    )
    ads = lax.dynamic_index_in_dim(
        ad_embedding.reshape(NZ, NS, SHARD, -1), my_block(), 1, keepdims=False
    ).reshape(ADS_HERE, -1)
    pot_parts = over_planes(pot_parts)
    pair = lax.all_gather(message, "c")
    behind = {
        d: lax.ppermute(pair, "y", [(i, i ^ d) for i in range(NY)]) for d in (1, 2, 3)
    }
    messages = [pair, behind[1], behind[3], behind[2]]
    demand = listing_view_demand.reshape(ADS_J // 128, 128)
    penalty = listing_unplaced_penalty.reshape(ADS_J // 128, 128)

    tile, row_parts, mass, pot = call(
        tile_kernel,
        [(ADS_HERE, USERS_HERE), (NROW, NS, UBS), (NS, UBS), (1, ADS_HERE)],
        *messages, ads, ad_scale.reshape(ADS_J // 128, 128) * WEIGHT, pot_parts,
        scratch=[(NS, UBS)],
    )
    row_pot, col_parts = call(
        first_column_kernel,
        [(NS, UBS), (NZ, 1, ADS_HERE)],
        tile, over_rows(row_parts), mass, pot,
    )
    pot, row_parts, fallback, log_demand = call(
        second_row_kernel,
        [(1, ADS_HERE), (NROW, NS, UBS), (1, ADS_HERE), (1, ADS_HERE)],
        tile, over_planes(col_parts), row_pot, pot, penalty, demand,
        scratch=[(NS, UBS)],
    )
    new_row_pot, col_parts = call(
        second_column_kernel,
        [(NS, UBS), (NZ, 1, ADS_HERE)],
        tile, over_rows(row_parts), row_pot, mass, pot,
    )
    last, users = call(
        last_kernel,
        [(1, SHARD), (1, UBS)],
        over_planes(col_parts), pot, fallback, log_demand, new_row_pot,
    )
    return users.reshape(UBS), last.reshape(SHARD)


def solution(mesh):
    fine = Mesh(mesh.devices.reshape(NZ, NY, NC, NX), ("z", "y", "c", "x"))
    user = ("z", "y", "c")
    in_specs = (
        P(user, None),
        P(user),
        P(user),
        P("x", None),
        P("x"),
        P("x"),
        P("x"),
        P(("x",) + user),
        P(user, "x", None),
        P(user, "x"),
    )
    out_specs = (P(user), P(("x",) + user))
    return jax.shard_map(
        on_device, mesh=fine, in_specs=in_specs, out_specs=out_specs, check_vma=False
    )
```
